256 devices in a mesh: dp: 4 (over y_hi, core), ctx: 8 (over z), tp: 8 (over y_lo, x).
Axes of the slice: x: 4, y: 4 (y_hi: 2, y_lo: 2; y = y_hi * 2 + y_lo), z: 8, core: 2. Of those that a mesh axis runs over, the one named last changes fastest.
Arguments:
- q_lat: bfloat16 [4, 1536, 128, 512], P('dp', 'ctx', 'tp'), may hold values from -36 to 36
- q_rope: bfloat16 [4, 1536, 8192], P('dp', 'ctx', 'tp'), may hold values from -4 to 4
- latent: bfloat16 [4, 1536, 512], P('dp', ('ctx', 'tp')), may hold values from -4 to 4
- k_rope: bfloat16 [4, 1536, 64], P('dp', ('ctx', 'tp')), may hold values from -4 to 4
- d_out: bfloat16 [4, 1536, 16384], P('dp', 'ctx', 'tp'), may hold values from -0.078125 to 0.078125
- w_uv: bfloat16 [128, 512, 128], P('tp'), may hold values from -0.25 to 0.25
- doc_lengths: int32 [4, 8], P('dp'), may hold values from 1 to 384, 1536 in all within a row
- block_order: int32 [4, 24], P('dp'), may hold values from 0 to 23, as said below
Outputs:
- attn_out: bfloat16 [4, 1536, 16384], P('dp', 'ctx', 'tp')
- grad_uv: float32 [512, 128, 128], P(('dp', 'ctx'), 'tp')
The draws below stay inside these ranges and needn't reach their ends.
Inputs may be any that keep to these rules, and one draw needn't show every extreme that they name: `block_order`: each row is a permutation of the block numbers 0 to 23; the index k of ctx holds the blocks listed at places k * 3 to (k+1) * 3 - 1.
All inputs are finite; a program needn't handle non-finite values.
Results may differ from the reference program's by a relative error of at most 0.0052.
Values may be sent and summed in bfloat16 or wider, within the bound.
A program may use at most 128 MiB of HBM per device.

```python
import math
import jax
import jax.numpy as jnp
import numpy as np
from jax import lax

H = 128
LAT = 512
ROPE = 64
NOPE = 128
VD = 128
TOK_DEV = 192
BLOCK = 64
NDOC = 8
WINDOWS = 4
WINDOW = 1536
NBLOCK = 24
DOC_MAX = 384
N_DP = 4
N_CTX = 8


def window_order(key):
    keys = jax.random.split(jax.random.fold_in(key, 101), WINDOWS)
    return jax.vmap(lambda single: jax.random.permutation(single, NBLOCK))(keys).astype(jnp.int32)


def window_latent(key):
    raw = jax.random.normal(jax.random.fold_in(key, 102), (WINDOWS, WINDOW, LAT), jnp.float32)
    return jnp.clip(raw, -4.0, 4.0)


def draw_block_order(key, part):
    return window_order(key)


def draw_latent(key, part):
    return window_latent(key).astype(jnp.bfloat16)


def draw_q_lat(key, part):
    key = jax.random.fold_in(key, 3)
    noise = jnp.clip(jax.random.normal(key, (WINDOWS, WINDOW, H, LAT), jnp.float32), -4.0, 4.0)
    return noise.astype(jnp.bfloat16)


def level_of(stream_key, dims, cuts, smallest, top_value):
    level, own = 1.0, jax.random.fold_in(stream_key, 6)
    for dim, parts in cuts:
        heights = jnp.exp(jax.random.uniform(jax.random.fold_in(own, dim), (parts,), jnp.float32, smallest / len(cuts), top_value / len(cuts)))
        level = level * jnp.repeat(heights, dims[dim] // parts).reshape([-1 if axis == dim else 1 for axis in range(len(dims))])
    return level


def profile(number_of, total, limit, skew):
    loads = [(1 << 20) // math.isqrt(standing ** skew) + 1 for standing in range(2, number_of + 1)]
    rest, given = total - limit - (number_of - 1), [1] * (number_of - 1)
    while rest > 0:
        candidates = [i for i in range(number_of - 1) if given[i] < limit]
        whole, budget = sum([loads[i] for i in candidates]), rest
        for i in candidates:
            addition = min(limit - given[i], max(1, budget * loads[i] // whole), rest)
            given[i] = given[i] + addition
            rest = rest - addition
    return np.array([limit] + given)


def uneven_parts(key, amount, total, most, lean):
    if amount == 2:
        one = jax.random.randint(key, (), max(1, total - most), min(most, total - 1) + 1)
        return jnp.stack([one, total - one])
    sizes = jnp.asarray(profile(amount, total, most, lean), jnp.int32)
    twos = (amount - 1) // 2
    source_of, sink = sizes[1:1 + 2 * twos:2], sizes[2:2 + 2 * twos:2]
    slack = jnp.minimum(source_of - 1, most - sink)
    passed = jax.random.randint(jax.random.fold_in(key, 1), (twos,), 0, 1 << 20) % (slack + 1)
    sizes = sizes.at[1:1 + 2 * twos:2].set(source_of - passed).at[2:2 + 2 * twos:2].set(sink + passed)
    return sizes[jax.random.permutation(jax.random.fold_in(key, 2), amount)]


def bell_draw(own_key, dims, deviation, most, cuts=(), kind=jnp.bfloat16):
    loudness = level_of(own_key, dims, cuts, -0.22, 0.18) if cuts else 1.0
    drawn = jax.random.normal(own_key, dims, jnp.float32) * deviation * loudness
    return jnp.minimum(jnp.maximum(drawn, -most), most).astype(kind)


def setup_inputs(seed: int = 0) -> dict:
    seeds = jax.random.split(jax.random.key(seed), 9)
    q_lat = draw_q_lat(jax.random.fold_in(seeds[8], 71), 0)
    q_rope = bell_draw(seeds[1], (WINDOWS, WINDOW, H * ROPE), 1.0, 4.0, ((0, 4), (1, 8), (2, 8)))
    latent = draw_latent(jax.random.fold_in(seeds[8], 71), 0)
    k_rope = bell_draw(seeds[3], (WINDOWS, WINDOW, ROPE), 1.0, 4.0, ((0, 4), (1, 64)))
    d_out = bell_draw(seeds[4], (WINDOWS, WINDOW, H * VD), (TOK_DEV * N_CTX * N_DP) ** -0.5, 0.078125, ((0, 4), (1, 8), (2, 8)))
    w_uv = bell_draw(seeds[5], (H, LAT, VD), LAT ** -0.5, 0.25, ((0, 8),))
    doc_lengths = jax.vmap(lambda own: uneven_parts(own, NDOC, WINDOW, DOC_MAX, 2))(jax.random.split(seeds[6], WINDOWS)).reshape((WINDOWS, NDOC)).astype(jnp.int32)
    block_order = draw_block_order(jax.random.fold_in(seeds[8], 71), 0)
    return {"q_lat": q_lat, "q_rope": q_rope, "latent": latent, "k_rope": k_rope, "d_out": d_out, "w_uv": w_uv, "doc_lengths": doc_lengths, "block_order": block_order}


def document_index(positions, ends):
    return jnp.sum((positions[:, None] >= ends[None, :]).astype(jnp.int32), axis=1).astype(jnp.int32)


def reference(q_lat, q_rope, latent, k_rope, d_out, w_uv, doc_lengths, block_order):
    span = DOC_MAX + BLOCK
    factor = (NOPE + ROPE) ** -0.5
    offsets = jnp.arange(BLOCK, dtype=jnp.int32)
    reach = jnp.arange(span, dtype=jnp.int32)
    weights_uv = w_uv.astype(jnp.float32)
    highest = lax.Precision.HIGHEST
    grad = jnp.zeros((LAT, H, VD), jnp.float32)
    outputs = []
    for window in range(WINDOWS):
        ends = jnp.cumsum(doc_lengths[window]).astype(jnp.int32)
        keys_lat = latent[window].astype(jnp.float32)
        keys_rope = k_rope[window].astype(jnp.float32)
        order = block_order[window]
        queries_lat = q_lat[window]
        queries_rope = q_rope[window]
        cotangent = d_out[window]

        def step(carry, slot):
            zero = jnp.zeros((), jnp.int32)
            block_id = order[slot].astype(jnp.int32)
            start = (slot * BLOCK).astype(jnp.int32)
            qlat = lax.dynamic_slice(queries_lat, (start, zero, zero), (BLOCK, H, LAT)).astype(jnp.float32)
            qrope = lax.dynamic_slice(queries_rope, (start, zero), (BLOCK, H * ROPE)).astype(jnp.float32).reshape(BLOCK, H, ROPE)
            grads_out = lax.dynamic_slice(cotangent, (start, zero), (BLOCK, H * VD)).astype(jnp.float32).reshape(BLOCK, H, VD)
            query_pos = block_id * BLOCK + offsets
            first = jnp.maximum(block_id * BLOCK + BLOCK - span, 0).astype(jnp.int32)
            klat = lax.dynamic_slice(keys_lat, (first, zero), (span, LAT))
            krope = lax.dynamic_slice(keys_rope, (first, zero), (span, ROPE))
            key_pos = first + reach
            scores = jnp.einsum("rhc,nc->hrn", qlat, klat, precision=highest)
            scores = scores + jnp.einsum("rhc,nc->hrn", qrope, krope, precision=highest)
            scores = scores * factor
            same_doc = document_index(query_pos, ends)[:, None] == document_index(key_pos, ends)[None, :]
            allowed = same_doc & (key_pos[None, :] <= query_pos[:, None])
            scores = jnp.where(allowed[None], scores, -jnp.inf)
            top = jnp.max(scores, axis=2, keepdims=True)
            probs = jnp.exp(scores - top)
            total = jnp.sum(probs, axis=2)
            rounded = lax.optimization_barrier(probs.astype(jnp.bfloat16))
            mixed = jnp.einsum("hrn,nc->rhc", rounded.astype(jnp.float32), klat, precision=highest)
            mixed = lax.optimization_barrier((mixed / jnp.transpose(total)[:, :, None]).astype(jnp.bfloat16))
            mixed_wide = mixed.astype(jnp.float32)
            attn = jnp.einsum("rhc,hcv->rhv", mixed_wide, weights_uv, precision=highest).astype(jnp.bfloat16)
            carry = carry + jnp.einsum("rhc,rhv->chv", mixed_wide, grads_out, precision=highest)
            return carry, attn

        grad, attn_rows = lax.scan(step, grad, jnp.arange(NBLOCK, dtype=jnp.int32))
        outputs.append(attn_rows.reshape(WINDOW, H * VD))
    return jnp.stack(outputs, axis=0), grad
```

```python
import math
import jax
import jax.numpy as jnp
from jax import lax
from jax.experimental import pallas as pl
from jax.experimental.pallas import tpu as pltpu
from jax.sharding import PartitionSpec as P

MESH = pl.DeviceIdType.MESH
NG = 4

class Gather:
    def __init__(self, keys, send, recv):
        self.keys, self.send, self.recv = keys, send, recv
        self.z = lax.axis_index("ctx")
        tp = lax.axis_index("tp")
        self.y, self.x = tp // 4, tp % 4
        self.yp = lax.axis_index("dp") % 2
        self.yq = 1 - self.yp

    def X(self, d): return (self.x + d + 4) % 4
    def Z(self, d): return (self.z + d + 8) % 8

    def to(self, slot):
        if slot < 8: return {"tp": ((self.y + slot // 4) % 2) * 4 + self.X(slot % 4)}
        return {"ctx": self.Z(slot - 7)}

    def copy(self, z, y, x, slot):
        i = (z * 2 + y) * 4 + x
        r = self.keys.at[pl.ds(i * 3, 3)]
        return pltpu.make_async_remote_copy(src_ref=r, dst_ref=r, send_sem=self.send.at[slot, i], recv_sem=self.recv.at[i], device_id=self.to(slot), device_id_type=MESH)

    def put(self, z, y, x, slots):
        for s in slots: self.copy(z, y, x, s).start()

    def arrive(self, z, y, x):
        self.copy(z, y, x, 1).wait_recv()

    def sent(self, z, y, x, slots):
        for s in slots: self.copy(z, y, x, s).wait_send()

    def barrier(self):
        b = pltpu.get_barrier_semaphore()
        for s in range(1, 15):
            pl.semaphore_signal(b, inc=1, device_id=self.to(s), device_id_type=MESH)
        pl.semaphore_wait(b, 14)

    PLANE = (4, 1, 3, 5, 7, 2, 6)
    LINE = (8, 14, 9, 13, 10, 12, 11)
    UP, DOWN = 8, 14

    def run(self):
        x, y, z, yp, yq = self.x, self.y, self.z, self.yp, self.yq
        @pl.when(y == yp)
        def _():
            self.put(z, yp, x, (self.UP, self.DOWN) + self.PLANE)
        @pl.when(y == yq)
        def _():
            self.put(z, yq, x, self.LINE)
            self.put(z, yq, x, self.PLANE)
            self.arrive(z, yp, x)
            self.put(z, yp, x, (self.UP, self.DOWN))
        for dx in (1, 3, 2):
            self.arrive(z, yp, self.X(dx))
            self.put(z, yp, self.X(dx), (self.UP, self.DOWN))
        for d in (1, 2, 3, 4):
            for k, dx in enumerate((0, 1, 3, 2)):
                for s, zz in ((self.UP, self.Z(-d)), (self.DOWN, self.Z(d))):
                    mine = s == (self.UP, self.DOWN)[k % 2]
                    if d == 4 and not mine: continue
                    self.arrive(zz, yp, self.X(dx))
                    if d < 3 or (d == 3 and mine): self.put(zz, yp, self.X(dx), (s,))
            if d < 3:
                @pl.when(y == yq)
                def _():
                    for dz in ((1, -1, 2, -2), (3, -3, 4))[d - 1]:
                        self.arrive(self.Z(dz), yq, x)
                        self.put(self.Z(dz), yq, x, self.PLANE)
        @pl.when(y == yp)
        def _():
            for dz in (0, 1, -1, 2, -2, 3, -3, 4): self.arrive(self.Z(dz), yq, x)
        for dz in (0, 1, -1, 2, -2, 3, -3, 4):
            for dx in (1, 3, 2): self.arrive(self.Z(dz), yq, self.X(dx))

    def drain(self):
        x, y, z, yp, yq = self.x, self.y, self.z, self.yp, self.yq
        @pl.when(y == yp)
        def _():
            self.sent(z, yp, x, self.PLANE)
        @pl.when(y == yq)
        def _():
            self.sent(z, yq, x, self.LINE)
            for dz in range(8): self.sent(dz, yq, x, self.PLANE)
        for k, dx in enumerate((0, 1, 3, 2)):
            self.sent(z, yp, self.X(dx), (self.UP, self.DOWN))
            for d in (1, 2, 3):
                for s, zz in ((self.UP, self.Z(-d)), (self.DOWN, self.Z(d))):
                    mine = s == (self.UP, self.DOWN)[k % 2]
                    if d < 3 or mine: self.sent(zz, yp, self.X(dx), (s,))

def gather_kernel(lat, rope, out, keys, send, recv):
    g = Gather(keys, send, recv)
    i = (g.z * 2 + g.y) * 4 + g.x
    r = jnp.concatenate([rope[0], rope[0]], axis=1)
    for t in range(3):
        keys[i * 3 + t, :, 0:512] = lat[0, t*8:(t+1)*8, :]
        keys[i * 3 + t, :, 512:640] = r[t*8:(t+1)*8, :]
    g.barrier()
    g.run()
    g.drain()
    out[...] = keys[...]

def gather(lat, rope):
    V=pl.BlockSpec(memory_space=pltpu.VMEM)
    return pl.pallas_call(gather_kernel, out_shape=jax.ShapeDtypeStruct((192, 8, 640), jnp.bfloat16), in_specs=[V, V], out_specs=V,
        scratch_shapes=[pltpu.VMEM((192, 8, 640), jnp.bfloat16), pltpu.SemaphoreType.DMA((15, 64)), pltpu.SemaphoreType.DMA((64,))],
        compiler_params=pltpu.CompilerParams(collective_id=0, has_side_effects=True, vmem_limit_bytes=50<<20), name="gather")(lat, rope)

BLOCK=64; SPAN=448; GH=4
SCALE = 192.0 ** -0.5 * math.log2(math.e)

def start_of_doc(pos, dl):
    end = jnp.int32(0); lo = jnp.zeros_like(pos)
    for d in range(8):
        n = dl[0, d]; end = end + n
        lo = lo + jnp.where(pos >= end, n, 0)
    return lo

def compute_kernel(bo, dl, q_ref, qr_ref, do_ref, w_ref, k_ref, attn_ref, grad_ref, qt, bias, u):
    place = lax.axis_index("ctx")
    keys = k_ref.reshape(1536, 640)
    lane = lax.broadcasted_iota(jnp.int32, (64, 128), 1)
    for b in range(3):
        for c in range(4):
            x = q_ref[0, b*64:(b+1)*64, :, c*128:(c+1)*128]
            qt[b, :, :, c*128:(c+1)*128] = jnp.swapaxes(x, 0, 1)
        for j in range(8):
            pair = qr_ref[0, b*64:(b+1)*64, j*128:(j+1)*128]
            z = jnp.zeros_like(pair)
            qt[b, 2*j, :, 512:640] = jnp.where(lane < 64, pair, z)
            qt[b, 2*j+1, :, 512:640] = jnp.where(lane < 64, z, pair)
    firsts=[]
    for b in range(3):
        blk = bo[0, place*3+b]
        first = jnp.maximum(blk-6, 0)*64
        firsts.append(pl.multiple_of(first, 64))
        p = blk*64 + lax.broadcasted_iota(jnp.int32, (64, 1), 0)
        lo = start_of_doc(p, dl)
        j = first + lax.broadcasted_iota(jnp.int32, (64, SPAN), 1)
        bias[b] = jnp.where((j >= lo) & (j <= p), 0.0, -1e30)
    def group(g, _):
        for b in range(3):
            q = qt[b, pl.ds(g*GH, GH)].reshape(GH*64, 640)
            k = keys[pl.ds(firsts[b], SPAN), :]
            s = lax.dot_general(q, k, (((1,),(1,)),((),())), preferred_element_type=jnp.float32)
            s = s.reshape(GH, 64, SPAN) + bias[b][None]
            m = jnp.max(s, axis=2, keepdims=True)
            p = jnp.exp2((s - m) * SCALE)
            t = jnp.sum(p, axis=2, keepdims=True)
            pb = p.astype(jnp.bfloat16).reshape(GH*64, SPAN)
            mixed = lax.dot_general(pb, k[:, :512], (((1,),(0,)),((),())), preferred_element_type=jnp.float32)
            u[:, b*64:(b+1)*64, :] = (mixed.reshape(GH, 64, 512) / t).astype(jnp.bfloat16)
        for i in range(GH):
            h = g*GH+i
            uh = u[i]
            col = pl.ds(pl.multiple_of(h*128, 128), 128)
            attn_ref[0, :, col] = jnp.dot(uh, w_ref[h], preferred_element_type=jnp.float32).astype(jnp.bfloat16)
            gr = lax.dot_general(uh, do_ref[0, :, col], (((0,),(0,)),((),())), preferred_element_type=jnp.float32)
            grad_ref[h] = gr
        return 0
    lax.fori_loop(0, 16//GH, group, 0)

def compute(bo, dl, q, qr, do, w, k):
    V=pl.BlockSpec(memory_space=pltpu.VMEM); S=pl.BlockSpec(memory_space=pltpu.SMEM)
    return pl.pallas_call(compute_kernel,
      out_shape=[jax.ShapeDtypeStruct((1,192,2048), jnp.bfloat16), jax.ShapeDtypeStruct((16,512,128), jnp.float32)],
      in_specs=[S,S,V,V,V,V,V], out_specs=[V,V],
      scratch_shapes=[pltpu.VMEM((3,16,64,640),jnp.bfloat16), pltpu.VMEM((3,64,SPAN),jnp.float32), pltpu.VMEM((GH,192,512),jnp.bfloat16)],
      compiler_params=pltpu.CompilerParams(vmem_limit_bytes=50<<20), name="compute")(bo, dl, q, qr, do, w, k)

class Reduce:
    def __init__(self, grad, cs, cr, ys, yr, zs, zr, own, fin, sems):
        self.grad, self.cs, self.cr, self.ys, self.yr, self.zs, self.zr, self.own, self.fin = grad, cs, cr, ys, yr, zs, zr, own, fin
        self.csem, self.ysem, self.zssem, self.zrsem = sems
        self.z = lax.axis_index("ctx")
        dp = lax.axis_index("dp")
        self.hi, self.core = dp // 2, dp % 2

    def Z(self, d): return (self.z + d + 8) % 8
    def sibling(self): return {"dp": self.hi * 2 + 1 - self.core}
    def across(self): return {"dp": (1 - self.hi) * 2 + self.core}

    def targets(self):
        return [self.sibling(), self.across()] + [{"ctx": self.Z(d)} for d in range(1, 8)]

    def c_copy(self, g):
        return pltpu.make_async_remote_copy(src_ref=self.cs.at[g], dst_ref=self.cr.at[g], send_sem=self.csem.at[0, g], recv_sem=self.csem.at[1, g], device_id=self.sibling(), device_id_type=MESH)
    def y_copy(self, g):
        return pltpu.make_async_remote_copy(src_ref=self.ys.at[g], dst_ref=self.yr.at[g], send_sem=self.ysem.at[0, g], recv_sem=self.ysem.at[1, g], device_id=self.across(), device_id_type=MESH)
    def z_copy(self, g, d):
        return pltpu.make_async_remote_copy(src_ref=self.zs.at[g, self.Z(d)], dst_ref=self.zr.at[g, d - 1], send_sem=self.zssem.at[g, d - 1], recv_sem=self.zrsem.at[g, d - 1], device_id={"ctx": self.Z(d)}, device_id_type=MESH)

    def rows(self, g, i, hi, core):
        start = pl.multiple_of((hi * 2 + core) * 128, 128)
        return self.grad[g * GH + i, pl.ds(start, 128), :].reshape(8, 16, 128)

    def a(self, g):
        for hi in range(2):
            for i in range(GH):
                self.cs[g, hi, :, i] = self.rows(g, i, hi, 1 - self.core).astype(jnp.bfloat16)
        self.c_copy(g).start()

    def b(self, g):
        self.c_copy(g).wait_recv()
        for i in range(GH):
            v = self.rows(g, i, 1 - self.hi, self.core) + self.cr[g, 1 - self.hi, :, i].astype(jnp.float32)
            self.ys[g, :, i] = v.astype(jnp.bfloat16)
        self.y_copy(g).start()
        for i in range(GH):
            self.own[g, :, i] = self.rows(g, i, self.hi, self.core) + self.cr[g, self.hi, :, i].astype(jnp.float32)

    def c(self, g):
        self.y_copy(g).wait_recv()
        v = self.own[g] + self.yr[g].astype(jnp.float32)
        self.own[g] = v
        self.zs[g] = v.astype(jnp.bfloat16)
        for d in (4, 3, 5, 2, 6, 1, 7): self.z_copy(g, d).start()

    def d(self, g):
        total = self.own[g, self.z]
        for d in (1, 7, 2, 6, 3, 5, 4):
            self.z_copy(g, d).wait_recv()
            total = total + self.zr[g, d - 1].astype(jnp.float32)
        self.fin[pl.ds(g * GH, GH)] = total

    def drain(self):
        for g in range(NG):
            self.c_copy(g).wait_send(); self.y_copy(g).wait_send()
            for d in range(1, 8): self.z_copy(g, d).wait_send()

    def scratch():
        return [pltpu.VMEM((NG, 2, 8, GH, 16, 128), jnp.bfloat16), pltpu.VMEM((NG, 2, 8, GH, 16, 128), jnp.bfloat16),
          pltpu.VMEM((NG, 8, GH, 16, 128), jnp.bfloat16), pltpu.VMEM((NG, 8, GH, 16, 128), jnp.bfloat16),
          pltpu.VMEM((NG, 8, GH, 16, 128), jnp.bfloat16), pltpu.VMEM((NG, 7, GH, 16, 128), jnp.bfloat16),
          pltpu.VMEM((NG, 8, GH, 16, 128), jnp.float32), pltpu.VMEM((16, 16, 128), jnp.float32),
          pltpu.SemaphoreType.DMA((2, NG)), pltpu.SemaphoreType.DMA((2, NG)), pltpu.SemaphoreType.DMA((NG, 7)), pltpu.SemaphoreType.DMA((NG, 7))]

def reduce_kernel(grad, out, *s):
    r = Reduce(grad, *s[:8], s[8:])
    b = pltpu.get_barrier_semaphore()
    for t in r.targets(): pl.semaphore_signal(b, inc=1, device_id=t, device_id_type=MESH)
    pl.semaphore_wait(b, 9)
    stages = (r.a, r.b, r.c, r.d)
    for t in range(NG + 3):
        for k in (3, 2, 1, 0):
            if 0 <= t - k < NG: stages[k](t - k)
    r.drain()
    out[...] = jnp.swapaxes(r.fin[...], 0, 1)

def reduce(grad):
    V=pl.BlockSpec(memory_space=pltpu.VMEM)
    return pl.pallas_call(reduce_kernel, out_shape=jax.ShapeDtypeStruct((16, 16, 128), jnp.float32), in_specs=[V], out_specs=V,
        scratch_shapes=Reduce.scratch(),
        compiler_params=pltpu.CompilerParams(collective_id=1, has_side_effects=True, vmem_limit_bytes=50<<20), name="reduce")(grad)


def on_device(q_lat, q_rope, latent, k_rope, d_out, w_uv, doc_lengths, block_order):
    keys = gather(latent, k_rope)
    attn, grad = compute(block_order, doc_lengths, q_lat, q_rope, d_out, w_uv, keys)
    return attn, reduce(grad)


def solution(mesh):
    return jax.shard_map(
        on_device,
        mesh=mesh,
        in_specs=(
            P("dp", "ctx", "tp", None),
            P("dp", "ctx", "tp"),
            P("dp", ("ctx", "tp"), None),
            P("dp", ("ctx", "tp"), None),
            P("dp", "ctx", "tp"),
            P("tp", None, None),
            P("dp", None),
            P("dp", None),
        ),
        out_specs=(P("dp", "ctx", "tp"), P(("dp", "ctx"), "tp", None)),
        check_vma=False,
    )
```

```python
import math

import jax
import jax.numpy as jnp
from jax import lax
from jax.experimental import pallas as pl
from jax.experimental.pallas import tpu as pltpu
from jax.sharding import PartitionSpec as P

MESH = pl.DeviceIdType.MESH
BLOCK = 64
SPAN = 448
GH, NG = 4, 4
SCALE = 192.0**-0.5 * math.log2(math.e)


class Gather:
    def __init__(self, keys, send, recv):
        self.keys, self.send, self.recv = keys, send, recv
        self.z = lax.axis_index("ctx")
        tp = lax.axis_index("tp")
        self.y, self.x = tp // 4, tp % 4
        self.yp = lax.axis_index("dp") % 2
        self.yq = 1 - self.yp

    def X(self, d): return (self.x + d + 4) % 4
    def Z(self, d): return (self.z + d + 8) % 8

    def to(self, slot):
        if slot < 4: return {"tp": self.y * 4 + self.X(slot)}
        if slot == 4: return {"tp": (1 - self.y) * 4 + self.x}
        return {"ctx": self.Z(slot - 7)}

    ROW = (1, 3, 2)
    LINE = (8, 14, 9, 13, 10, 12, 11)
    UP, DOWN, UP2, DOWN2, ACROSS = 8, 14, 9, 13, 4
    Q, Q_ROW, P_LINE, P_ACROSS, COUNT = 32, 40, 41, 42, 43

    def copy(self, z, y, x, slot, arrival):
        r = self.keys.at[pl.ds(((z * 2 + y) * 4 + x) * 3, 3)]
        kind = 0 if slot < 4 else 1 if slot == 4 else 2
        return pltpu.make_async_remote_copy(src_ref=r, dst_ref=r, send_sem=self.send.at[kind], recv_sem=self.recv.at[arrival], device_id=self.to(slot), device_id_type=MESH)

    def put_p(self, z, x, slots, group=None):
        for s in slots: self.copy(z, self.yp, x, s, z * 4 + x if group is None else group).start()

    def put_q(self, z, slots, group=None):
        for s in slots: self.copy(z, self.yq, self.x, s, self.Q + z if group is None else group).start()

    def wait_p(self, z, x): self.copy(z, self.yp, x, 4, z * 4 + x).wait_recv()
    def wait_q(self, z): self.copy(z, self.yq, self.x, 4, self.Q + z).wait_recv()

    def many(self, shards, kind, arrival):
        r = self.keys.at[pl.ds(0, shards * 3)]
        return pltpu.make_async_remote_copy(src_ref=r, dst_ref=r, send_sem=self.send.at[kind], recv_sem=self.recv.at[arrival], device_id=self.to(4), device_id_type=MESH)

    def partners(self): return [self.to(s) for s in (1, 3, 2, 4) + self.LINE]

    def barrier(self):
        b = pltpu.get_barrier_semaphore()
        for t in self.partners(): pl.semaphore_signal(b, inc=1, device_id=t, device_id_type=MESH)
        pl.semaphore_wait(b, 11)

    def begin(self):
        x, z = self.x, self.z

        @pl.when(self.y == self.yp)
        def _():
            self.put_p(z, x, self.ROW)
            self.put_p(z, x, (self.ACROSS,))
            self.put_p(z, x, self.LINE, self.P_LINE)

        @pl.when(self.y == self.yq)
        def _():
            self.put_q(z, self.LINE)
            self.put_q(z, (self.ACROSS,))
            self.put_q(z, self.ROW, self.Q_ROW)

    def run(self):
        x, z = self.x, self.z
        X, Z = self.X, self.Z

        @pl.when(self.y == self.yp)
        def _():
            def near(dx):
                self.wait_p(z, X(dx))
                self.put_p(z, X(dx), (self.UP2, self.DOWN2, self.UP, self.DOWN))
                self.put_p(z, X(dx), (self.ACROSS,), self.P_ACROSS)
            def turn(dz):
                self.wait_q(Z(dz))
                self.put_q(Z(dz), self.ROW, self.Q_ROW)
            def over(dz, dx, slots=()):
                self.wait_p(Z(dz), X(dx))
                self.put_p(Z(dz), X(dx), slots)
                self.put_p(Z(dz), X(dx), (self.ACROSS,), self.P_ACROSS)
            near(1); near(3); turn(0); near(2)
            for k, dx in enumerate((1, 3, 2)):
                over(-2, dx, (self.UP, self.UP2) if k % 2 == 0 else (self.UP,))
                over(2, dx, (self.DOWN, self.DOWN2) if k % 2 == 1 else (self.DOWN,))
            turn(1); turn(-1)
            for dx in (1, 3, 2):
                over(1, dx); over(-1, dx)
            turn(2); turn(-2)
            turn(3); turn(-3); turn(4)
            for dx in (1, 3, 2):
                over(3, dx); over(-3, dx); over(4, dx)

        @pl.when(self.y == self.yq)
        def _():
            self.wait_p(z, x)
            self.put_p(z, x, self.LINE, self.P_LINE)
            for dz in (1, -1, 2, -2, 3, -3, 4):
                self.wait_q(Z(dz))
                self.put_q(Z(dz), (self.ACROSS,))
                self.put_q(Z(dz), self.ROW, self.Q_ROW)
            self.many(24, 0, self.P_ACROSS).wait_recv()

        self.many(7, 0, self.P_LINE).wait_recv()
        self.many(24, 0, self.Q_ROW).wait_recv()

    def drain(self):
        @pl.when(self.y == self.yp)
        def _():
            for kind, shards in enumerate((27, 25, 28)): self.many(shards, kind, 0).wait_send()
        @pl.when(self.y == self.yq)
        def _():
            for kind, shards in enumerate((24, 8, 14)): self.many(shards, kind, 0).wait_send()


class Reduce:
    def __init__(self, grad, cs, cr, ys, yr, zs, zr, own, fin, sems):
        self.grad, self.cs, self.cr, self.ys, self.yr, self.zs, self.zr, self.own, self.fin = grad, cs, cr, ys, yr, zs, zr, own, fin
        self.csem, self.ysem, self.zssem, self.zrsem = sems
        self.z = lax.axis_index("ctx")
        dp = lax.axis_index("dp")
        self.hi, self.core = dp // 2, dp % 2

    def Z(self, d): return (self.z + d + 8) % 8
    def sibling(self): return {"dp": self.hi * 2 + 1 - self.core}
    def across(self): return {"dp": (1 - self.hi) * 2 + self.core}

    def targets(self):
        return [self.sibling(), self.across()] + [{"ctx": self.Z(d)} for d in range(1, 8)]

    def c_copy(self, g):
        return pltpu.make_async_remote_copy(src_ref=self.cs.at[g], dst_ref=self.cr.at[g], send_sem=self.csem.at[0, g], recv_sem=self.csem.at[1, g], device_id=self.sibling(), device_id_type=MESH)
    def y_copy(self, g):
        return pltpu.make_async_remote_copy(src_ref=self.ys.at[g], dst_ref=self.yr.at[g], send_sem=self.ysem.at[0, g], recv_sem=self.ysem.at[1, g], device_id=self.across(), device_id_type=MESH)
    def z_copy(self, g, d):
        return pltpu.make_async_remote_copy(src_ref=self.zs.at[g, self.Z(d)], dst_ref=self.zr.at[g, d - 1], send_sem=self.zssem.at[g, d - 1], recv_sem=self.zrsem.at[g, d - 1], device_id={"ctx": self.Z(d)}, device_id_type=MESH)

    def rows(self, g, i, hi, core):
        start = pl.multiple_of((hi * 2 + core) * 128, 128)
        return self.grad[g * GH + i, pl.ds(start, 128), :].reshape(8, 16, 128)

    def a(self, g):
        for hi in range(2):
            for i in range(GH):
                self.cs[g, hi, :, i] = self.rows(g, i, hi, 1 - self.core).astype(jnp.bfloat16)
        self.c_copy(g).start()

    def b(self, g):
        self.c_copy(g).wait_recv()
        for i in range(GH):
            v = self.rows(g, i, 1 - self.hi, self.core) + self.cr[g, 1 - self.hi, :, i].astype(jnp.float32)
            self.ys[g, :, i] = v.astype(jnp.bfloat16)
        self.y_copy(g).start()
        for i in range(GH):
            self.own[g, :, i] = self.rows(g, i, self.hi, self.core) + self.cr[g, self.hi, :, i].astype(jnp.float32)

    def c(self, g):
        self.y_copy(g).wait_recv()
        v = self.own[g] + self.yr[g].astype(jnp.float32)
        self.own[g] = v
        self.zs[g] = v.astype(jnp.bfloat16)
        for d in (4, 3, 5, 2, 6, 1, 7): self.z_copy(g, d).start()

    def d(self, g):
        total = self.own[g, self.z]
        for d in (1, 7, 2, 6, 3, 5, 4):
            self.z_copy(g, d).wait_recv()
            total = total + self.zr[g, d - 1].astype(jnp.float32)
        self.fin[pl.ds(g * GH, GH)] = total

    def drain(self):
        for g in range(NG):
            self.c_copy(g).wait_send(); self.y_copy(g).wait_send()
            for d in range(1, 8): self.z_copy(g, d).wait_send()

    def scratch():
        return [pltpu.VMEM((NG, 2, 8, GH, 16, 128), jnp.bfloat16), pltpu.VMEM((NG, 2, 8, GH, 16, 128), jnp.bfloat16),
          pltpu.VMEM((NG, 8, GH, 16, 128), jnp.bfloat16), pltpu.VMEM((NG, 8, GH, 16, 128), jnp.bfloat16),
          pltpu.VMEM((NG, 8, GH, 16, 128), jnp.bfloat16), pltpu.VMEM((NG, 7, GH, 16, 128), jnp.bfloat16),
          pltpu.VMEM((NG, 8, GH, 16, 128), jnp.float32), pltpu.VMEM((16, 16, 128), jnp.float32),
          pltpu.SemaphoreType.DMA((2, NG)), pltpu.SemaphoreType.DMA((2, NG)), pltpu.SemaphoreType.DMA((NG, 7)), pltpu.SemaphoreType.DMA((NG, 7))]


def start_of_doc(pos, lengths):
    end, low = jnp.int32(0), jnp.zeros_like(pos)
    for d in range(8):
        n = lengths[0, d]
        end = end + n
        low = low + jnp.where(pos >= end, n, 0)
    return low


class Attend:
    def __init__(self, order, lengths, q, qr, qt, keys, bias, u):
        self.order, self.lengths, self.q, self.qr, self.qt, self.keys, self.bias, self.u = order, lengths, q, qr, qt, keys, bias, u
        self.firsts = []

    def arrange(self):
        lane = lax.broadcasted_iota(jnp.int32, (BLOCK, 128), 1)
        for b in range(3):
            rows = slice(b * BLOCK, (b + 1) * BLOCK)
            for c in range(4):
                cols = slice(c * 128, (c + 1) * 128)
                self.qt[b, :, :, cols] = jnp.swapaxes(self.q[0, rows, :, cols], 0, 1)
            for j in range(8):
                pair = self.qr[0, rows, j * 128 : (j + 1) * 128]
                zero = jnp.zeros_like(pair)
                self.qt[b, 2 * j, :, 512:640] = jnp.where(lane < 64, pair, zero)
                self.qt[b, 2 * j + 1, :, 512:640] = jnp.where(lane < 64, zero, pair)

    def mask(self):
        place = lax.axis_index("ctx")
        for b in range(3):
            block = self.order[0, place * 3 + b]
            first = jnp.maximum(block - 6, 0) * BLOCK
            self.firsts.append(jnp.maximum(block - 6, 0) * 8)
            pos = block * BLOCK + lax.broadcasted_iota(jnp.int32, (BLOCK, 1), 0)
            low = start_of_doc(pos, self.lengths)
            j = first + lax.broadcasted_iota(jnp.int32, (BLOCK, SPAN), 1)
            self.bias[b] = jnp.where((j >= low) & (j <= pos), 0.0, -1e30)

    def block(self, g, b):
        q = self.qt[b, pl.ds(g * GH, GH)].reshape(GH * BLOCK, 640)
        k = self.keys[pl.ds(self.firsts[b], SPAN // 8)].reshape(SPAN, 640)
        s = lax.dot_general(q, k, (((1,), (1,)), ((), ())), preferred_element_type=jnp.float32)
        s = s.reshape(GH, BLOCK, SPAN) + self.bias[b][None]
        top = jnp.max(s, axis=2, keepdims=True)
        p = jnp.exp2((s - top) * SCALE)
        total = jnp.sum(p, axis=2, keepdims=True)
        weights = p.astype(jnp.bfloat16).reshape(GH * BLOCK, SPAN)
        mixed = lax.dot_general(weights, k[:, :512], (((1,), (0,)), ((), ())), preferred_element_type=jnp.float32)
        self.u[pl.ds(g * GH, GH), b * BLOCK : (b + 1) * BLOCK, :] = (mixed.reshape(GH, BLOCK, 512) / total).astype(jnp.bfloat16)


def kernel(order_hbm, lengths_hbm, lat_hbm, rope_hbm, q_hbm, qr_hbm, do_hbm, w_hbm, attn, out, order, lengths, lat, rope, q, qr, do, w, loads, keys, send, recv, qt, bias, u, grad, *reduce_refs):
    copies = [
        pltpu.make_async_copy(src, dst, loads.at[i])
        for i, (src, dst) in enumerate(
            ((lat_hbm, lat), (rope_hbm, rope), (order_hbm, order), (lengths_hbm, lengths), (q_hbm, q), (qr_hbm, qr), (do_hbm, do), (w_hbm, w))
        )
    ]
    for c in copies:
        c.start()
    g = Gather(keys, send, recv)
    r = Reduce(grad, *reduce_refs[:8], reduce_refs[8:])
    barrier = pltpu.get_barrier_semaphore()
    partners = g.partners() + r.targets()[:2]
    for t in partners:
        pl.semaphore_signal(barrier, inc=1, device_id=t, device_id_type=MESH)
    copies[0].wait()
    copies[1].wait()
    mine = ((g.z * 2 + g.y) * 4 + g.x) * 3
    twice = jnp.concatenate([rope[0], rope[0]], axis=1)
    for t in range(3):
        keys[mine + t, :, 0:512] = lat[0, t * 8 : (t + 1) * 8, :]
        keys[mine + t, :, 512:640] = twice[t * 8 : (t + 1) * 8, :]
    pl.semaphore_wait(barrier, len(partners))
    g.begin()
    for c in copies[2:]:
        c.wait()
    a = Attend(order, lengths, q, qr, qt, keys, bias, u)
    a.arrange()
    a.mask()
    g.run()

    def group(i, _):
        a.block(i, 0)
        pl.when(i >= 1)(lambda: r.b(i - 1))
        a.block(i, 1)
        pl.when(i >= 2)(lambda: r.c(i - 2))
        a.block(i, 2)
        pl.when(i >= 3)(lambda: r.d(i - 3))
        for h in range(GH):
            head = i * GH + h
            col = pl.ds(pl.multiple_of(head * 128, 128), 128)
            grad[head] = lax.dot_general(u[head], do[0, :, col], (((0,), (0,)), ((), ())), preferred_element_type=jnp.float32)
        r.a(i)
        return 0

    lax.fori_loop(0, NG, group, 0)

    def values(i):
        def head(h, _):
            col = pl.ds(pl.multiple_of(h * 128, 128), 128)
            attn[0, :, col] = jnp.dot(u[h], w[h], preferred_element_type=jnp.float32).astype(jnp.bfloat16)
            return 0

        lax.fori_loop(i * GH, (i + 1) * GH, head, 0)

    values(0)
    r.b(3)
    r.c(2)
    r.d(1)
    values(1)
    values(2)
    r.c(3)
    values(3)
    r.d(2)
    r.d(3)
    out[...] = jnp.swapaxes(r.fin[...], 0, 1)
    g.drain()
    r.drain()


def on_device(q_lat, q_rope, latent, k_rope, d_out, w_uv, doc_lengths, block_order):
    hbm = pl.BlockSpec(memory_space=pltpu.HBM)
    vmem = pl.BlockSpec(memory_space=pltpu.VMEM)
    operands = (block_order, doc_lengths, latent, k_rope, q_lat, q_rope, d_out, w_uv)
    return pl.pallas_call(
        kernel,
        out_shape=[jax.ShapeDtypeStruct((1, 192, 2048), jnp.bfloat16), jax.ShapeDtypeStruct((16, 16, 128), jnp.float32)],
        in_specs=[hbm] * 8,
        out_specs=[vmem, vmem],
        scratch_shapes=[
            pltpu.SMEM((1, 24), jnp.int32),
            pltpu.SMEM((1, 8), jnp.int32),
            *(pltpu.VMEM(x.shape, x.dtype) for x in operands[2:]),
            pltpu.SemaphoreType.DMA((8,)),
            pltpu.VMEM((192, 8, 640), jnp.bfloat16),
            pltpu.SemaphoreType.DMA((3,)),
            pltpu.SemaphoreType.DMA((Gather.COUNT,)),
            pltpu.VMEM((3, 16, BLOCK, 640), jnp.bfloat16),
            pltpu.VMEM((3, BLOCK, SPAN), jnp.float32),
            pltpu.VMEM((16, 192, 512), jnp.bfloat16),
            pltpu.VMEM((16, 512, 128), jnp.float32),
            *Reduce.scratch(),
        ],
        compiler_params=pltpu.CompilerParams(collective_id=0, has_side_effects=True, vmem_limit_bytes=56 << 20),
        name="attention",
    )(*operands)


def solution(mesh):
    return jax.shard_map(
        on_device,
        mesh=mesh,
        in_specs=(
            P("dp", "ctx", "tp", None),
            P("dp", "ctx", "tp"),
            P("dp", ("ctx", "tp"), None),
            P("dp", ("ctx", "tp"), None),
            P("dp", "ctx", "tp"),
            P("tp", None, None),
            P("dp", None),
            P("dp", None),
        ),
        out_specs=(P("dp", "ctx", "tp"), P(("dp", "ctx"), "tp", None)),
        check_vma=False,
    )
```

```python
import math

import jax
import jax.numpy as jnp
from jax import lax
from jax.experimental import pallas as pl
from jax.experimental.pallas import tpu as pltpu
from jax.sharding import PartitionSpec as P

MESH = pl.DeviceIdType.MESH
BLOCK = 64
SPAN = 448
GH = 4
UH, NU = 2, 8
Z_FIRST = (0, 4)
Y_FIRST = tuple(u for u in range(NU) if u not in Z_FIRST)
VMEM_MB = 56
SCALE = 192.0**-0.5 * math.log2(math.e)


class Gather:
    def __init__(self, keys, send, recv):
        self.keys, self.send, self.recv = keys, send, recv
        self.z = lax.axis_index("ctx")
        tp = lax.axis_index("tp")
        self.y, self.x = tp // 4, tp % 4
        self.yp = lax.axis_index("dp") % 2
        self.yq = 1 - self.yp

    def X(self, d): return (self.x + d + 4) % 4
    def Z(self, d): return (self.z + d + 8) % 8

    def to(self, slot):
        if slot < 4: return {"tp": self.y * 4 + self.X(slot)}
        if slot == 4: return {"tp": (1 - self.y) * 4 + self.x}
        return {"ctx": self.Z(slot - 7)}

    ROW = (1, 3, 2)
    LINE = (8, 14, 9, 13, 10, 12, 11)
    UP, DOWN, UP2, DOWN2, ACROSS = 8, 14, 9, 13, 4
    Q, Q_ROW, P_LINE, P_ACROSS, COUNT = 32, 40, 41, 42, 43

    def copy(self, z, y, x, slot, arrival):
        r = self.keys.at[pl.ds(((z * 2 + y) * 4 + x) * 3, 3)]
        kind = 0 if slot < 4 else 1 if slot == 4 else 2
        return pltpu.make_async_remote_copy(src_ref=r, dst_ref=r, send_sem=self.send.at[kind], recv_sem=self.recv.at[arrival], device_id=self.to(slot), device_id_type=MESH)

    def put_p(self, z, x, slots, group=None):
        for s in slots: self.copy(z, self.yp, x, s, z * 4 + x if group is None else group).start()

    def put_q(self, z, slots, group=None):
        for s in slots: self.copy(z, self.yq, self.x, s, self.Q + z if group is None else group).start()

    def wait_p(self, z, x): self.copy(z, self.yp, x, 4, z * 4 + x).wait_recv()
    def wait_q(self, z): self.copy(z, self.yq, self.x, 4, self.Q + z).wait_recv()

    def many(self, shards, kind, arrival):
        r = self.keys.at[pl.ds(0, shards * 3)]
        return pltpu.make_async_remote_copy(src_ref=r, dst_ref=r, send_sem=self.send.at[kind], recv_sem=self.recv.at[arrival], device_id=self.to(4), device_id_type=MESH)

    def partners(self): return [self.to(s) for s in (1, 3, 2, 4) + self.LINE]

    def barrier(self):
        b = pltpu.get_barrier_semaphore()
        for t in self.partners(): pl.semaphore_signal(b, inc=1, device_id=t, device_id_type=MESH)
        pl.semaphore_wait(b, 11)

    def begin(self):
        x, z = self.x, self.z

        @pl.when(self.y == self.yp)
        def _():
            self.put_p(z, x, self.ROW)
            self.put_p(z, x, (self.ACROSS,))
            self.put_p(z, x, self.LINE, self.P_LINE)

        @pl.when(self.y == self.yq)
        def _():
            self.put_q(z, self.LINE)
            self.put_q(z, (self.ACROSS,))
            self.put_q(z, self.ROW, self.Q_ROW)

    def run(self):
        x, z = self.x, self.z
        X, Z = self.X, self.Z

        @pl.when(self.y == self.yp)
        def _():
            def near(dx):
                self.wait_p(z, X(dx))
                self.put_p(z, X(dx), (self.UP2, self.DOWN2, self.UP, self.DOWN))
                self.put_p(z, X(dx), (self.ACROSS,), self.P_ACROSS)
            def turn(dz):
                self.wait_q(Z(dz))
                self.put_q(Z(dz), self.ROW, self.Q_ROW)
            def over(dz, dx, slots=()):
                self.wait_p(Z(dz), X(dx))
                self.put_p(Z(dz), X(dx), slots)
                self.put_p(Z(dz), X(dx), (self.ACROSS,), self.P_ACROSS)
            near(1); near(3); turn(0); near(2)
            for k, dx in enumerate((1, 3, 2)):
                over(-2, dx, (self.UP, self.UP2) if k % 2 == 0 else (self.UP,))
                over(2, dx, (self.DOWN, self.DOWN2) if k % 2 == 1 else (self.DOWN,))
            turn(1); turn(-1)
            for dx in (1, 3, 2):
                over(1, dx); over(-1, dx)
            turn(2); turn(-2)
            turn(3); turn(-3); turn(4)
            for dx in (1, 3, 2):
                over(3, dx); over(-3, dx); over(4, dx)

        @pl.when(self.y == self.yq)
        def _():
            self.wait_p(z, x)
            self.put_p(z, x, self.LINE, self.P_LINE)
            for dz in (1, -1, 2, -2, 3, -3, 4):
                self.wait_q(Z(dz))
                self.put_q(Z(dz), (self.ACROSS,))
                self.put_q(Z(dz), self.ROW, self.Q_ROW)
            self.many(24, 0, self.P_ACROSS).wait_recv()

        self.many(7, 0, self.P_LINE).wait_recv()
        self.many(24, 0, self.Q_ROW).wait_recv()

    def drain(self):
        @pl.when(self.y == self.yp)
        def _():
            for kind, shards in enumerate((27, 25, 28)): self.many(shards, kind, 0).wait_send()
        @pl.when(self.y == self.yq)
        def _():
            for kind, shards in enumerate((24, 8, 14)): self.many(shards, kind, 0).wait_send()


class Reduce:
    def __init__(self, grad, fin, cs, cr, ys, yr, zs, zr, zs2, zr2, ys2, yr2, acc, sent, csem, ysem, zsem):
        self.grad, self.fin, self.cs, self.cr, self.ys, self.yr, self.zs, self.zr = grad, fin, cs, cr, ys, yr, zs, zr
        self.zs2, self.zr2, self.ys2, self.yr2, self.acc = zs2, zr2, ys2, yr2, acc
        self.sem, self.csem, self.ysem, self.zsem = sent, csem, ysem, zsem
        self.z = lax.axis_index("ctx")
        dp = lax.axis_index("dp")
        self.hi, self.core = dp // 2, dp % 2

    FAR_FIRST = (4, 3, 5, 2, 6, 1, 7)

    def Z(self, d):
        return (self.z + d + 8) % 8

    def sibling(self):
        return {"dp": self.hi * 2 + 1 - self.core}

    def across(self):
        return {"dp": (1 - self.hi) * 2 + self.core}

    def copy(self, src, dst, kind, recv, to):
        return pltpu.make_async_remote_copy(
            src_ref=src, dst_ref=dst, send_sem=self.sem.at[kind], recv_sem=recv, device_id=to, device_id_type=MESH
        )

    def bufs(self, u):
        if u in Z_FIRST:
            k = Z_FIRST.index(u)
            return self.ys2.at[k], self.yr2.at[k], self.zs2.at[k], self.zr2.at[k]
        k = Y_FIRST.index(u)
        return self.ys.at[k], self.yr.at[k], self.zs.at[k], self.zr.at[k]

    def c_copy(self, u):
        return self.copy(self.cs.at[u], self.cr.at[u], 0, self.csem.at[u], self.sibling())

    def y_copy(self, u):
        ys, yr, _, _ = self.bufs(u)
        return self.copy(ys, yr, 3 if u in Z_FIRST else 1, self.ysem.at[u], self.across())

    def z_start(self, u):
        _, _, zs, zr = self.bufs(u)
        for d in self.FAR_FIRST:
            self.copy(zs.at[self.Z(d)], zr.at[d - 1], 4 if u in Z_FIRST else 2, self.zsem.at[u], {"ctx": self.Z(d)}).start()

    def z_wait(self, u):
        _, _, _, zr = self.bufs(u)
        self.copy(zr, zr, 2, self.zsem.at[u], self.across()).wait_recv()

    def rows(self, u, i, hi, core):
        start = pl.multiple_of((hi * 2 + core) * 128, 128)
        return self.grad[u * UH + i, pl.ds(start, 128), :].reshape(8, 16, 128)

    def both(self, u, i, hi):
        return self.rows(u, i, hi, self.core) + self.cr[u, hi, :, i].astype(jnp.float32)

    def mine(self, u, i, hi):
        start = pl.multiple_of((hi * 2 + self.core) * 128 + self.z * 16, 16)
        return self.grad[u * UH + i, pl.ds(start, 16), :] + self.cr[u, hi, self.z, i].astype(jnp.float32)

    def a(self, u):
        for hi in range(2):
            for i in range(UH):
                self.cs[u, hi, :, i] = self.rows(u, i, hi, 1 - self.core).astype(jnp.bfloat16)
        self.c_copy(u).start()

    def b(self, u):
        self.c_copy(u).wait_recv()
        ys, _, zs, _ = self.bufs(u)
        for i in range(UH):
            if u in Z_FIRST:
                for hi in range(2):
                    zs[:, hi, i] = self.both(u, i, hi).astype(jnp.bfloat16)
            else:
                ys[:, i] = self.both(u, i, 1 - self.hi).astype(jnp.bfloat16)
        if u in Z_FIRST:
            self.z_start(u)
        else:
            self.y_copy(u).start()

    def c(self, u):
        ys, yr, zs, zr = self.bufs(u)
        if u in Z_FIRST:
            self.z_wait(u)
            k = Z_FIRST.index(u)
            for i in range(UH):
                for far in range(2):
                    hi = 1 - self.hi if far else self.hi
                    total = self.mine(u, i, hi)
                    for d in range(7):
                        total = total + zr[d, hi, i].astype(jnp.float32)
                    if far:
                        ys[i] = total.astype(jnp.bfloat16)
                    else:
                        self.acc[k, i] = total
            self.y_copy(u).start()
        else:
            self.y_copy(u).wait_recv()
            for i in range(UH):
                zs[:, i] = (self.both(u, i, self.hi) + yr[:, i].astype(jnp.float32)).astype(jnp.bfloat16)
            self.z_start(u)

    def d(self, u):
        _, yr, _, zr = self.bufs(u)
        if u in Z_FIRST:
            self.y_copy(u).wait_recv()
        else:
            self.z_wait(u)
        for i in range(UH):
            if u in Z_FIRST:
                total = self.acc[Z_FIRST.index(u), i] + yr[i].astype(jnp.float32)
            else:
                total = self.mine(u, i, self.hi) + yr[self.z, i].astype(jnp.float32)
                for d in range(7):
                    total = total + zr[d, i].astype(jnp.float32)
            self.fin[u * UH + i] = total

    def drain(self):
        for kind, whole in enumerate((self.cs, self.ys, self.zr, self.ys2, self.zr2)):
            self.copy(whole, whole, kind, self.csem.at[0], self.across()).wait_send()

    def scratch():
        tile, half = (UH, 16, 128), (2, UH, 16, 128)
        ny, nz = len(Y_FIRST), len(Z_FIRST)
        shapes = [(NU, 2, 8) + tile] * 2 + [(ny, 8) + tile] * 3 + [(ny, 7) + tile, (nz, 8) + half, (nz, 7) + half, (nz,) + tile, (nz,) + tile]
        return [
            pltpu.VMEM((16, 16, 128), jnp.float32),
            *(pltpu.VMEM(shape, jnp.bfloat16) for shape in shapes),
            pltpu.VMEM((nz,) + tile, jnp.float32),
            pltpu.SemaphoreType.DMA((5,)),
            *[pltpu.SemaphoreType.DMA((NU,))] * 3,
        ]


def start_of_doc(pos, lengths):
    end, low = jnp.int32(0), jnp.zeros_like(pos)
    for d in range(8):
        n = lengths[0, d]
        end = end + n
        low = low + jnp.where(pos >= end, n, 0)
    return low


class Attend:
    def __init__(self, order, lengths, q, qr, qt, keys, bias, u):
        self.order, self.lengths, self.q, self.qr, self.qt, self.keys, self.bias, self.u = order, lengths, q, qr, qt, keys, bias, u
        self.firsts = []

    def arrange(self):
        lane = lax.broadcasted_iota(jnp.int32, (BLOCK, 128), 1)
        for b in range(3):
            rows = slice(b * BLOCK, (b + 1) * BLOCK)
            for c in range(4):
                cols = slice(c * 128, (c + 1) * 128)
                self.qt[b, :, :, cols] = jnp.swapaxes(self.q[0, rows, :, cols], 0, 1)
            for j in range(8):
                pair = self.qr[0, rows, j * 128 : (j + 1) * 128]
                zero = jnp.zeros_like(pair)
                self.qt[b, 2 * j, :, 512:640] = jnp.where(lane < 64, pair, zero)
                self.qt[b, 2 * j + 1, :, 512:640] = jnp.where(lane < 64, zero, pair)

    def mask(self):
        place = lax.axis_index("ctx")
        for b in range(3):
            block = self.order[0, place * 3 + b]
            first = jnp.maximum(block - 6, 0) * BLOCK
            self.firsts.append(jnp.maximum(block - 6, 0) * 8)
            pos = block * BLOCK + lax.broadcasted_iota(jnp.int32, (BLOCK, 1), 0)
            low = start_of_doc(pos, self.lengths)
            j = first + lax.broadcasted_iota(jnp.int32, (BLOCK, SPAN), 1)
            self.bias[b] = jnp.where((j >= low) & (j <= pos), 0.0, -1e30)

    def block(self, head, n, b):
        q = self.qt[b, pl.ds(head, n)].reshape(n * BLOCK, 640)
        k = self.keys[pl.ds(self.firsts[b], SPAN // 8)].reshape(SPAN, 640)
        s = lax.dot_general(q, k, (((1,), (1,)), ((), ())), preferred_element_type=jnp.float32)
        s = s.reshape(n, BLOCK, SPAN) + self.bias[b][None]
        top = jnp.max(s, axis=2, keepdims=True)
        p = jnp.exp2((s - top) * SCALE)
        total = jnp.sum(p, axis=2, keepdims=True)
        weights = p.astype(jnp.bfloat16).reshape(n * BLOCK, SPAN)
        mixed = lax.dot_general(weights, k[:, :512], (((1,), (0,)), ((), ())), preferred_element_type=jnp.float32)
        self.u[pl.ds(head, n), b * BLOCK : (b + 1) * BLOCK, :] = (mixed.reshape(n, BLOCK, 512) / total).astype(jnp.bfloat16)


def kernel(order_hbm, lengths_hbm, lat_hbm, rope_hbm, q_hbm, qr_hbm, do_hbm, w_hbm, attn, out, order, lengths, lat, rope, q, qr, do, w, loads, keys, send, recv, qt, bias, u, grad, *reduce_refs):
    copies = [
        pltpu.make_async_copy(src, dst, loads.at[i])
        for i, (src, dst) in enumerate(
            ((lat_hbm, lat), (rope_hbm, rope), (order_hbm, order), (lengths_hbm, lengths), (q_hbm, q), (qr_hbm, qr), (do_hbm, do), (w_hbm, w))
        )
    ]
    for c in copies:
        c.start()
    g = Gather(keys, send, recv)
    r = Reduce(grad, *reduce_refs)
    barrier = pltpu.get_barrier_semaphore()
    partners = g.partners() + [r.sibling(), r.across()]
    for t in partners:
        pl.semaphore_signal(barrier, inc=1, device_id=t, device_id_type=MESH)
    copies[0].wait()
    copies[1].wait()
    mine = ((g.z * 2 + g.y) * 4 + g.x) * 3
    twice = jnp.concatenate([rope[0], rope[0]], axis=1)
    for t in range(3):
        keys[mine + t, :, 0:512] = lat[0, t * 8 : (t + 1) * 8, :]
        keys[mine + t, :, 512:640] = twice[t * 8 : (t + 1) * 8, :]
    pl.semaphore_wait(barrier, len(partners))
    g.begin()
    for c in copies[2:]:
        c.wait()
    a = Attend(order, lengths, q, qr, qt, keys, bias, u)
    a.arrange()
    a.mask()
    g.run()

    def gradient(first, n):
        for h in range(n):
            col = pl.ds(pl.multiple_of((first + h) * 128, 128), 128)
            grad[first + h] = lax.dot_general(u[first + h], do[0, :, col], (((0,), (0,)), ((), ())), preferred_element_type=jnp.float32)

    def group(first, n, work, units):
        for b in range(3):
            a.block(first, n, b)
            for act, u in work[b]:
                act(u)
        gradient(first, n)
        for u in units:
            r.a(u)

    none = ()
    group(0, 8, (none, none, none), (2, 0, 3, 1))
    group(8, 8, (((r.b, 2), (r.b, 0), (r.b, 3), (r.b, 1)), none, none), (5, 4, 6, 7))

    def values(i):
        def head(h, _):
            col = pl.ds(pl.multiple_of(h * 128, 128), 128)
            attn[0, :, col] = jnp.dot(u[h], w[h], preferred_element_type=jnp.float32).astype(jnp.bfloat16)
            return 0

        lax.fori_loop(i * GH, (i + 1) * GH, head, 0)

    values(0)
    for unit in (5, 4, 6, 7):
        r.b(unit)
    for unit in (2, 3):
        r.c(unit)
    values(1)
    for unit in (5, 0, 1):
        r.c(unit)
    values(2)
    for unit in (6, 7, 4):
        r.c(unit)
    values(3)
    for unit in (2, 3, 5, 0, 1, 6, 4, 7):
        r.d(unit)
    out[...] = jnp.swapaxes(r.fin[...], 0, 1)
    g.drain()
    r.drain()


def on_device(q_lat, q_rope, latent, k_rope, d_out, w_uv, doc_lengths, block_order):
    hbm = pl.BlockSpec(memory_space=pltpu.HBM)
    vmem = pl.BlockSpec(memory_space=pltpu.VMEM)
    operands = (block_order, doc_lengths, latent, k_rope, q_lat, q_rope, d_out, w_uv)
    return pl.pallas_call(
        kernel,
        out_shape=[pltpu.VMEM((1, 192, 2048), jnp.bfloat16), pltpu.VMEM((16, 16, 128), jnp.float32)],
        in_specs=[hbm] * 8,
        out_specs=[vmem, vmem],
        scratch_shapes=[
            pltpu.SMEM((1, 24), jnp.int32),
            pltpu.SMEM((1, 8), jnp.int32),
            *(pltpu.VMEM(x.shape, x.dtype) for x in operands[2:]),
            pltpu.SemaphoreType.DMA((8,)),
            pltpu.VMEM((192, 8, 640), jnp.bfloat16),
            pltpu.SemaphoreType.DMA((3,)),
            pltpu.SemaphoreType.DMA((Gather.COUNT,)),
            pltpu.VMEM((3, 16, BLOCK, 640), jnp.bfloat16),
            pltpu.VMEM((3, BLOCK, SPAN), jnp.float32),
            pltpu.VMEM((16, 192, 512), jnp.bfloat16),
            pltpu.VMEM((16, 512, 128), jnp.float32),
            *Reduce.scratch(),
        ],
        compiler_params=pltpu.CompilerParams(collective_id=0, has_side_effects=True, vmem_limit_bytes=VMEM_MB << 20),
        name="attention",
    )(*operands)


def solution(mesh):
    return jax.shard_map(
        on_device,
        mesh=mesh,
        in_specs=(
            P("dp", "ctx", "tp", None),
            P("dp", "ctx", "tp"),
            P("dp", ("ctx", "tp"), None),
            P("dp", ("ctx", "tp"), None),
            P("dp", "ctx", "tp"),
            P("tp", None, None),
            P("dp", None),
            P("dp", None),
        ),
        out_specs=(P("dp", "ctx", "tp"), P(("dp", "ctx"), "tp", None)),
        check_vma=False,
    )
```

```python
import math

import jax
import jax.numpy as jnp
from jax import lax
from jax.experimental import pallas as pl
from jax.experimental.pallas import tpu as pltpu
from jax.sharding import PartitionSpec as P

MESH = pl.DeviceIdType.MESH
BLOCK = 64
SPAN = 448
GH = 4
UH, NU = 2, 8
Z_FIRST = (0, 3)
Y_FIRST = tuple(u for u in range(NU) if u not in Z_FIRST)
VMEM_MB = 56
SCALE = 192.0**-0.5 * math.log2(math.e)


class Gather:
    def __init__(self, keys, send, recv):
        self.keys, self.send, self.recv = keys, send, recv
        self.z = lax.axis_index("ctx")
        tp = lax.axis_index("tp")
        self.y, self.x = tp // 4, tp % 4
        self.yp = lax.axis_index("dp") % 2
        self.yq = 1 - self.yp

    def X(self, d): return (self.x + d + 4) % 4
    def Z(self, d): return (self.z + d + 8) % 8

    def to(self, slot):
        if slot < 4: return {"tp": self.y * 4 + self.X(slot)}
        if slot == 4: return {"tp": (1 - self.y) * 4 + self.x}
        return {"ctx": self.Z(slot - 7)}

    ROW = (1, 3, 2)
    LINE = (8, 14, 9, 13, 10, 12, 11)
    UP, DOWN, UP2, DOWN2, ACROSS = 8, 14, 9, 13, 4
    Q, Q_ROW, P_LINE, P_ACROSS, COUNT = 32, 40, 41, 42, 43

    def copy(self, z, y, x, slot, arrival):
        r = self.keys.at[pl.ds(((z * 2 + y) * 4 + x) * 3, 3)]
        kind = 0 if slot < 4 else 1 if slot == 4 else 2
        return pltpu.make_async_remote_copy(src_ref=r, dst_ref=r, send_sem=self.send.at[kind], recv_sem=self.recv.at[arrival], device_id=self.to(slot), device_id_type=MESH)

    def put_p(self, z, x, slots, group=None):
        for s in slots: self.copy(z, self.yp, x, s, z * 4 + x if group is None else group).start()

    def put_q(self, z, slots, group=None):
        for s in slots: self.copy(z, self.yq, self.x, s, self.Q + z if group is None else group).start()

    def wait_p(self, z, x): self.copy(z, self.yp, x, 4, z * 4 + x).wait_recv()
    def wait_q(self, z): self.copy(z, self.yq, self.x, 4, self.Q + z).wait_recv()

    def many(self, shards, kind, arrival):
        r = self.keys.at[pl.ds(0, shards * 3)]
        return pltpu.make_async_remote_copy(src_ref=r, dst_ref=r, send_sem=self.send.at[kind], recv_sem=self.recv.at[arrival], device_id=self.to(4), device_id_type=MESH)

    def partners(self): return [self.to(s) for s in (1, 3, 2, 4) + self.LINE]

    def barrier(self):
        b = pltpu.get_barrier_semaphore()
        for t in self.partners(): pl.semaphore_signal(b, inc=1, device_id=t, device_id_type=MESH)
        pl.semaphore_wait(b, 11)

    def begin(self):
        x, z = self.x, self.z

        @pl.when(self.y == self.yp)
        def _():
            self.put_p(z, x, self.ROW)
            self.put_p(z, x, (self.ACROSS,))
            self.put_p(z, x, (self.UP2, self.DOWN2))
            self.put_p(z, x, (self.UP, self.DOWN), self.P_LINE)

        @pl.when(self.y == self.yq)
        def _():
            self.put_q(z, self.LINE)
            self.put_q(z, (self.ACROSS,))
            self.put_q(z, self.ROW, self.Q_ROW)

    def run(self):
        x, z = self.x, self.z
        X, Z = self.X, self.Z

        def hop(up, down):
            self.wait_p(Z(-2), x)
            self.put_p(Z(-2), x, up, self.P_LINE)
            self.wait_p(Z(2), x)
            self.put_p(Z(2), x, down, self.P_LINE)

        @pl.when(self.y == self.yp)
        def _():
            def near(dx):
                self.wait_p(z, X(dx))
                self.put_p(z, X(dx), (self.UP2, self.DOWN2, self.UP, self.DOWN))
                self.put_p(z, X(dx), (self.ACROSS,), self.P_ACROSS)
            def turn(dz):
                self.wait_q(Z(dz))
                self.put_q(Z(dz), self.ROW, self.Q_ROW)
            def over(dz, dx, slots=()):
                self.wait_p(Z(dz), X(dx))
                self.put_p(Z(dz), X(dx), slots)
                self.put_p(Z(dz), X(dx), (self.ACROSS,), self.P_ACROSS)
            near(1); near(3); near(2)
            hop((self.UP, self.UP2), (self.DOWN,))
            turn(0); turn(1); turn(-1)
            over(-2, 1, (self.UP, self.UP2)); over(2, 1, (self.DOWN,))
            over(-2, 3, (self.UP,)); over(2, 3, (self.DOWN, self.DOWN2))
            turn(2); turn(-2)
            over(-2, 2, (self.UP, self.UP2)); over(2, 2, (self.DOWN,))
            for dx in (1, 3, 2):
                over(1, dx); over(-1, dx)
            turn(3); turn(-3); turn(4)
            for dx in (1, 3, 2):
                over(3, dx); over(-3, dx); over(4, dx)

        @pl.when(self.y == self.yq)
        def _():
            def cross(dz):
                self.wait_q(Z(dz))
                self.put_q(Z(dz), (self.ACROSS,))
                self.put_q(Z(dz), self.ROW, self.Q_ROW)
            for dz in (1, -1, 2, -2):
                cross(dz)
            self.wait_p(z, x)
            self.put_p(z, x, (self.UP2, self.DOWN2))
            self.put_p(z, x, (self.UP, self.DOWN), self.P_LINE)
            for dz in (3, -3, 4):
                cross(dz)
            hop((self.UP,), (self.DOWN, self.DOWN2))
            self.many(24, 0, self.P_ACROSS).wait_recv()

        self.many(5, 0, self.P_LINE).wait_recv()
        self.many(24, 0, self.Q_ROW).wait_recv()

    def drain(self):
        @pl.when(self.y == self.yp)
        def _():
            for kind, shards in enumerate((27, 25, 28)): self.many(shards, kind, 0).wait_send()
        @pl.when(self.y == self.yq)
        def _():
            for kind, shards in enumerate((24, 8, 14)): self.many(shards, kind, 0).wait_send()


class Reduce:
    def __init__(self, grad, fin, cs, cr, ys, yr, zs, zr, zs2, zr2, ys2, yr2, acc, sent, csem, ysem, zsem):
        self.grad, self.fin, self.cs, self.cr, self.ys, self.yr, self.zs, self.zr = grad, fin, cs, cr, ys, yr, zs, zr
        self.zs2, self.zr2, self.ys2, self.yr2, self.acc = zs2, zr2, ys2, yr2, acc
        self.sem, self.csem, self.ysem, self.zsem = sent, csem, ysem, zsem
        self.z = lax.axis_index("ctx")
        dp = lax.axis_index("dp")
        self.hi, self.core = dp // 2, dp % 2

    FAR_FIRST = (4, 3, 5, 2, 6, 1, 7)

    def Z(self, d):
        return (self.z + d + 8) % 8

    def sibling(self):
        return {"dp": self.hi * 2 + 1 - self.core}

    def across(self):
        return {"dp": (1 - self.hi) * 2 + self.core}

    def copy(self, src, dst, kind, recv, to):
        return pltpu.make_async_remote_copy(
            src_ref=src, dst_ref=dst, send_sem=self.sem.at[kind], recv_sem=recv, device_id=to, device_id_type=MESH
        )

    def bufs(self, u):
        if u in Z_FIRST:
            k = Z_FIRST.index(u)
            return self.ys2.at[k], self.yr2.at[k], self.zs2.at[k], self.zr2.at[k]
        k = Y_FIRST.index(u)
        return self.ys.at[k], self.yr.at[k], self.zs.at[k], self.zr.at[k]

    def c_copy(self, u):
        return self.copy(self.cs.at[u], self.cr.at[u], 0, self.csem.at[u], self.sibling())

    def y_copy(self, u):
        ys, yr, _, _ = self.bufs(u)
        return self.copy(ys, yr, 3 if u in Z_FIRST else 1, self.ysem.at[u], self.across())

    def z_start(self, u):
        _, _, zs, zr = self.bufs(u)
        for d in self.FAR_FIRST:
            self.copy(zs.at[self.Z(d)], zr.at[d - 1], 4 if u in Z_FIRST else 2, self.zsem.at[u], {"ctx": self.Z(d)}).start()

    def z_wait(self, u):
        _, _, _, zr = self.bufs(u)
        self.copy(zr, zr, 2, self.zsem.at[u], self.across()).wait_recv()

    def rows(self, u, i, hi, core):
        start = pl.multiple_of((hi * 2 + core) * 128, 128)
        return self.grad[u * UH + i, pl.ds(start, 128), :].reshape(8, 16, 128)

    def both(self, u, i, hi):
        return self.rows(u, i, hi, self.core) + self.cr[u, hi, :, i].astype(jnp.float32)

    def mine(self, u, i, hi):
        start = pl.multiple_of((hi * 2 + self.core) * 128 + self.z * 16, 16)
        return self.grad[u * UH + i, pl.ds(start, 16), :] + self.cr[u, hi, self.z, i].astype(jnp.float32)

    def a(self, u):
        for hi in range(2):
            for i in range(UH):
                self.cs[u, hi, :, i] = self.rows(u, i, hi, 1 - self.core).astype(jnp.bfloat16)
        self.c_copy(u).start()

    def b(self, u):
        self.c_copy(u).wait_recv()
        ys, _, zs, _ = self.bufs(u)
        for i in range(UH):
            if u in Z_FIRST:
                for hi in range(2):
                    zs[:, hi, i] = self.both(u, i, hi).astype(jnp.bfloat16)
            else:
                ys[:, i] = self.both(u, i, 1 - self.hi).astype(jnp.bfloat16)
        if u in Z_FIRST:
            self.z_start(u)
        else:
            self.y_copy(u).start()

    def c(self, u):
        ys, yr, zs, zr = self.bufs(u)
        if u in Z_FIRST:
            self.z_wait(u)
            k = Z_FIRST.index(u)
            for i in range(UH):
                for far in range(2):
                    hi = 1 - self.hi if far else self.hi
                    total = self.mine(u, i, hi)
                    for d in range(7):
                        total = total + zr[d, hi, i].astype(jnp.float32)
                    if far:
                        ys[i] = total.astype(jnp.bfloat16)
                    else:
                        self.acc[k, i] = total
            self.y_copy(u).start()
        else:
            self.y_copy(u).wait_recv()
            for i in range(UH):
                zs[:, i] = (self.both(u, i, self.hi) + yr[:, i].astype(jnp.float32)).astype(jnp.bfloat16)
            self.z_start(u)

    def d(self, u):
        _, yr, _, zr = self.bufs(u)
        if u in Z_FIRST:
            self.y_copy(u).wait_recv()
        else:
            self.z_wait(u)
        for i in range(UH):
            if u in Z_FIRST:
                total = self.acc[Z_FIRST.index(u), i] + yr[i].astype(jnp.float32)
            else:
                total = self.mine(u, i, self.hi) + yr[self.z, i].astype(jnp.float32)
                for d in range(7):
                    total = total + zr[d, i].astype(jnp.float32)
            self.fin[u * UH + i] = total

    def drain(self):
        for kind, whole in enumerate((self.cs, self.ys, self.zr, self.ys2, self.zr2)):
            self.copy(whole, whole, kind, self.csem.at[0], self.across()).wait_send()

    def scratch():
        tile, half = (UH, 16, 128), (2, UH, 16, 128)
        ny, nz = len(Y_FIRST), len(Z_FIRST)
        shapes = [(NU, 2, 8) + tile] * 2 + [(ny, 8) + tile] * 3 + [(ny, 7) + tile, (nz, 8) + half, (nz, 7) + half, (nz,) + tile, (nz,) + tile]
        return [
            pltpu.VMEM((16, 16, 128), jnp.float32),
            *(pltpu.VMEM(shape, jnp.bfloat16) for shape in shapes),
            pltpu.VMEM((nz,) + tile, jnp.float32),
            pltpu.SemaphoreType.DMA((5,)),
            *[pltpu.SemaphoreType.DMA((NU,))] * 3,
        ]


def start_of_doc(pos, lengths):
    end, low = jnp.int32(0), jnp.zeros_like(pos)
    for d in range(8):
        n = lengths[0, d]
        end = end + n
        low = low + jnp.where(pos >= end, n, 0)
    return low


class Attend:
    def __init__(self, order, lengths, q, qr, qt, keys, bias, u):
        self.order, self.lengths, self.q, self.qr, self.qt, self.keys, self.bias, self.u = order, lengths, q, qr, qt, keys, bias, u
        self.firsts = []

    def arrange(self):
        lane = lax.broadcasted_iota(jnp.int32, (BLOCK, 128), 1)
        for b in range(3):
            rows = slice(b * BLOCK, (b + 1) * BLOCK)
            for c in range(4):
                cols = slice(c * 128, (c + 1) * 128)
                self.qt[b, :, :, cols] = jnp.swapaxes(self.q[0, rows, :, cols], 0, 1)
            for j in range(8):
                pair = self.qr[0, rows, j * 128 : (j + 1) * 128]
                zero = jnp.zeros_like(pair)
                self.qt[b, 2 * j, :, 512:640] = jnp.where(lane < 64, pair, zero)
                self.qt[b, 2 * j + 1, :, 512:640] = jnp.where(lane < 64, zero, pair)

    def mask(self):
        place = lax.axis_index("ctx")
        for b in range(3):
            block = self.order[0, place * 3 + b]
            first = jnp.maximum(block - 6, 0) * BLOCK
            self.firsts.append(jnp.maximum(block - 6, 0) * 8)
            pos = block * BLOCK + lax.broadcasted_iota(jnp.int32, (BLOCK, 1), 0)
            low = start_of_doc(pos, self.lengths)
            j = first + lax.broadcasted_iota(jnp.int32, (BLOCK, SPAN), 1)
            self.bias[b] = jnp.where((j >= low) & (j <= pos), 0.0, -1e30)

    def block(self, head, n, b):
        q = self.qt[b, pl.ds(head, n)].reshape(n * BLOCK, 640)
        k = self.keys[pl.ds(self.firsts[b], SPAN // 8)].reshape(SPAN, 640)
        s = lax.dot_general(q, k, (((1,), (1,)), ((), ())), preferred_element_type=jnp.float32)
        s = s.reshape(n, BLOCK, SPAN) + self.bias[b][None]
        top = jnp.max(s, axis=2, keepdims=True)
        p = jnp.exp2((s - top) * SCALE)
        total = jnp.sum(p, axis=2, keepdims=True)
        weights = p.astype(jnp.bfloat16).reshape(n * BLOCK, SPAN)
        mixed = lax.dot_general(weights, k[:, :512], (((1,), (0,)), ((), ())), preferred_element_type=jnp.float32)
        self.u[pl.ds(head, n), b * BLOCK : (b + 1) * BLOCK, :] = (mixed.reshape(n, BLOCK, 512) / total).astype(jnp.bfloat16)


def kernel(order_hbm, lengths_hbm, lat_hbm, rope_hbm, q_hbm, qr_hbm, do_hbm, w_hbm, attn, out, order, lengths, lat, rope, q, qr, do, w, loads, keys, send, recv, qt, bias, u, grad, *reduce_refs):
    copies = [
        pltpu.make_async_copy(src, dst, loads.at[i])
        for i, (src, dst) in enumerate(
            ((lat_hbm, lat), (rope_hbm, rope), (order_hbm, order), (lengths_hbm, lengths), (q_hbm, q), (qr_hbm, qr), (do_hbm, do), (w_hbm, w))
        )
    ]
    g = Gather(keys, send, recv)
    r = Reduce(grad, *reduce_refs)
    barrier = pltpu.get_barrier_semaphore()
    partners = g.partners() + [r.sibling(), r.across()]
    for t in partners:
        pl.semaphore_signal(barrier, inc=1, device_id=t, device_id_type=MESH)
    for c in copies:
        c.start()
    copies[0].wait()
    copies[1].wait()
    mine = ((g.z * 2 + g.y) * 4 + g.x) * 3
    twice = jnp.concatenate([rope[0], rope[0]], axis=1)
    for t in range(3):
        keys[mine + t, :, 0:512] = lat[0, t * 8 : (t + 1) * 8, :]
        keys[mine + t, :, 512:640] = twice[t * 8 : (t + 1) * 8, :]
    pl.semaphore_wait(barrier, len(partners))
    g.begin()
    for c in copies[2:]:
        c.wait()
    a = Attend(order, lengths, q, qr, qt, keys, bias, u)
    a.arrange()
    a.mask()
    g.run()

    def gradient(first, n):
        for h in range(n):
            col = pl.ds(pl.multiple_of((first + h) * 128, 128), 128)
            grad[first + h] = lax.dot_general(u[first + h], do[0, :, col], (((0,), (0,)), ((), ())), preferred_element_type=jnp.float32)

    def group(first, n, work, units):
        for b in range(3):
            a.block(first, n, b)
            for act, u in work[b]:
                act(u)
        gradient(first, n)
        for u in units:
            r.a(u)

    none = ()
    group(0, 6, (none, none, none), (1, 0, 2))
    group(6, 6, (((r.b, 1), (r.b, 0), (r.b, 2)), none, none), (4, 3, 5))
    group(12, 4, (none, ((r.b, 4), (r.b, 3), (r.b, 5)), none), (6, 7))

    def values(i):
        def head(h, _):
            col = pl.ds(pl.multiple_of(h * 128, 128), 128)
            attn[0, :, col] = jnp.dot(u[h], w[h], preferred_element_type=jnp.float32).astype(jnp.bfloat16)
            return 0

        lax.fori_loop(i * GH, (i + 1) * GH, head, 0)

    values(0)
    for unit in (6, 7):
        r.b(unit)
    for unit in (1, 2):
        r.c(unit)
    values(1)
    for unit in (0, 4, 5):
        r.c(unit)
    values(2)
    for unit in (6, 7, 3):
        r.c(unit)
    values(3)
    for unit in (1, 2, 4, 5, 0, 6, 3, 7):
        r.d(unit)
    out[...] = jnp.swapaxes(r.fin[...], 0, 1)
    g.drain()
    r.drain()


def on_device(q_lat, q_rope, latent, k_rope, d_out, w_uv, doc_lengths, block_order):
    hbm = pl.BlockSpec(memory_space=pltpu.HBM)
    vmem = pl.BlockSpec(memory_space=pltpu.VMEM)
    operands = (block_order, doc_lengths, latent, k_rope, q_lat, q_rope, d_out, w_uv)
    return pl.pallas_call(
        kernel,
        out_shape=[pltpu.VMEM((1, 192, 2048), jnp.bfloat16), pltpu.VMEM((16, 16, 128), jnp.float32)],
        in_specs=[hbm] * 8,
        out_specs=[vmem, vmem],
        scratch_shapes=[
            pltpu.SMEM((1, 24), jnp.int32),
            pltpu.SMEM((1, 8), jnp.int32),
            *(pltpu.VMEM(x.shape, x.dtype) for x in operands[2:]),
            pltpu.SemaphoreType.DMA((8,)),
            pltpu.VMEM((192, 8, 640), jnp.bfloat16),
            pltpu.SemaphoreType.DMA((3,)),
            pltpu.SemaphoreType.DMA((Gather.COUNT,)),
            pltpu.VMEM((3, 16, BLOCK, 640), jnp.bfloat16),
            pltpu.VMEM((3, BLOCK, SPAN), jnp.float32),
            pltpu.VMEM((16, 192, 512), jnp.bfloat16),
            pltpu.VMEM((16, 512, 128), jnp.float32),
            *Reduce.scratch(),
        ],
        compiler_params=pltpu.CompilerParams(collective_id=0, has_side_effects=True, vmem_limit_bytes=VMEM_MB << 20),
        name="attention",
    )(*operands)


def solution(mesh):
    return jax.shard_map(
        on_device,
        mesh=mesh,
        in_specs=(
            P("dp", "ctx", "tp", None),
            P("dp", "ctx", "tp"),
            P("dp", ("ctx", "tp"), None),
            P("dp", ("ctx", "tp"), None),
            P("dp", "ctx", "tp"),
            P("tp", None, None),
            P("dp", None),
            P("dp", None),
        ),
        out_specs=(P("dp", "ctx", "tp"), P(("dp", "ctx"), "tp", None)),
        check_vma=False,
    )
```

```python
import math

import jax
import jax.numpy as jnp
from jax import lax
from jax.experimental import pallas as pl
from jax.experimental.pallas import tpu as pltpu
from jax.sharding import PartitionSpec as P

MESH = pl.DeviceIdType.MESH
BLOCK = 64
SPAN = 448
GH = 4
UH, NU = 2, 8
Z_FIRST = (0, 3)
Y_FIRST = tuple(u for u in range(NU) if u not in Z_FIRST)
VMEM_MB = 56
SCALE = 192.0**-0.5 * math.log2(math.e)


class Gather:
    def __init__(self, keys, send, recv):
        self.keys, self.send, self.recv = keys, send, recv
        self.z = lax.axis_index("ctx")
        tp = lax.axis_index("tp")
        self.y, self.x = tp // 4, tp % 4
        self.yp = lax.axis_index("dp") % 2
        self.yq = 1 - self.yp

    def X(self, d): return (self.x + d + 4) % 4
    def Z(self, d): return (self.z + d + 8) % 8

    def to(self, slot):
        if slot < 4: return {"tp": self.y * 4 + self.X(slot)}
        if slot == 4: return {"tp": (1 - self.y) * 4 + self.x}
        return {"ctx": self.Z(slot - 7)}

    ROW = (1, 3, 2)
    LINE = (8, 14, 9, 13, 10, 12, 11)
    UP, DOWN, UP2, DOWN2, ACROSS = 8, 14, 9, 13, 4
    Q, Q_ROW, P_LINE, P_ACROSS, COUNT = 32, 40, 41, 42, 43

    def copy(self, z, y, x, slot, arrival):
        r = self.keys.at[pl.ds(((z * 2 + y) * 4 + x) * 3, 3)]
        kind = 0 if slot < 4 else 1 if slot == 4 else 2
        return pltpu.make_async_remote_copy(src_ref=r, dst_ref=r, send_sem=self.send.at[kind], recv_sem=self.recv.at[arrival], device_id=self.to(slot), device_id_type=MESH)

    def put_p(self, z, x, slots, group=None):
        for s in slots: self.copy(z, self.yp, x, s, z * 4 + x if group is None else group).start()

    def put_q(self, z, slots, group=None):
        for s in slots: self.copy(z, self.yq, self.x, s, self.Q + z if group is None else group).start()

    def wait_p(self, z, x): self.copy(z, self.yp, x, 4, z * 4 + x).wait_recv()
    def wait_q(self, z): self.copy(z, self.yq, self.x, 4, self.Q + z).wait_recv()

    def many(self, shards, kind, arrival):
        r = self.keys.at[pl.ds(0, shards * 3)]
        return pltpu.make_async_remote_copy(src_ref=r, dst_ref=r, send_sem=self.send.at[kind], recv_sem=self.recv.at[arrival], device_id=self.to(4), device_id_type=MESH)

    def partners(self): return [self.to(s) for s in (1, 3, 2, 4) + self.LINE]

    def barrier(self):
        b = pltpu.get_barrier_semaphore()
        for t in self.partners(): pl.semaphore_signal(b, inc=1, device_id=t, device_id_type=MESH)
        pl.semaphore_wait(b, 11)

    def begin(self):
        x, z = self.x, self.z

        @pl.when(self.y == self.yp)
        def _():
            self.put_p(z, x, self.ROW)
            self.put_p(z, x, (self.ACROSS,))
            self.put_p(z, x, (self.UP2, self.DOWN2))
            self.put_p(z, x, (self.UP, self.DOWN), self.P_LINE)

        @pl.when(self.y == self.yq)
        def _():
            self.put_q(z, self.LINE)
            self.put_q(z, (self.ACROSS,))
            self.put_q(z, self.ROW, self.Q_ROW)

    def run(self):
        x, z = self.x, self.z
        X, Z = self.X, self.Z

        def hop(up, down):
            self.wait_p(Z(-2), x)
            self.put_p(Z(-2), x, up, self.P_LINE)
            self.wait_p(Z(2), x)
            self.put_p(Z(2), x, down, self.P_LINE)

        @pl.when(self.y == self.yp)
        def _():
            def near(dx):
                self.wait_p(z, X(dx))
                self.put_p(z, X(dx), (self.UP2, self.DOWN2, self.UP, self.DOWN))
                self.put_p(z, X(dx), (self.ACROSS,), self.P_ACROSS)
            def turn(dz):
                self.wait_q(Z(dz))
                self.put_q(Z(dz), self.ROW, self.Q_ROW)
            def over(dz, dx, slots=()):
                self.wait_p(Z(dz), X(dx))
                self.put_p(Z(dz), X(dx), slots)
                self.put_p(Z(dz), X(dx), (self.ACROSS,), self.P_ACROSS)
            near(1); near(3); near(2)
            hop((self.UP, self.UP2), (self.DOWN,))
            turn(0); turn(1); turn(-1)
            over(-2, 1, (self.UP, self.UP2)); over(2, 1, (self.DOWN,))
            over(-2, 3, (self.UP,)); over(2, 3, (self.DOWN, self.DOWN2))
            turn(2); turn(-2)
            over(-2, 2, (self.UP, self.UP2)); over(2, 2, (self.DOWN,))
            for dx in (1, 3, 2):
                over(1, dx); over(-1, dx)
            turn(3); turn(-3); turn(4)
            for dx in (1, 3, 2):
                over(3, dx); over(-3, dx); over(4, dx)

        @pl.when(self.y == self.yq)
        def _():
            def cross(dz):
                self.wait_q(Z(dz))
                self.put_q(Z(dz), (self.ACROSS,))
                self.put_q(Z(dz), self.ROW, self.Q_ROW)
            for dz in (1, -1, 2, -2):
                cross(dz)
            self.wait_p(z, x)
            self.put_p(z, x, (self.UP2, self.DOWN2))
            self.put_p(z, x, (self.UP, self.DOWN), self.P_LINE)
            for dz in (3, -3, 4):
                cross(dz)
            hop((self.UP,), (self.DOWN, self.DOWN2))
            self.many(24, 0, self.P_ACROSS).wait_recv()

        self.many(5, 0, self.P_LINE).wait_recv()
        self.many(24, 0, self.Q_ROW).wait_recv()

    def drain(self):
        @pl.when(self.y == self.yp)
        def _():
            for kind, shards in enumerate((27, 25, 28)): self.many(shards, kind, 0).wait_send()
        @pl.when(self.y == self.yq)
        def _():
            for kind, shards in enumerate((24, 8, 14)): self.many(shards, kind, 0).wait_send()


class Reduce:
    def __init__(self, grad, fin, cs, cr, ys, yr, zs, zr, zs2, zr2, ys2, yr2, acc, sent, csem, ysem, zsem):
        self.grad, self.fin, self.cs, self.cr, self.ys, self.yr, self.zs, self.zr = grad, fin, cs, cr, ys, yr, zs, zr
        self.zs2, self.zr2, self.ys2, self.yr2, self.acc = zs2, zr2, ys2, yr2, acc
        self.sem, self.csem, self.ysem, self.zsem = sent, csem, ysem, zsem
        self.z = lax.axis_index("ctx")
        dp = lax.axis_index("dp")
        self.hi, self.core = dp // 2, dp % 2

    FAR_FIRST = (4, 3, 5, 2, 6, 1, 7)

    def Z(self, d):
        return (self.z + d + 8) % 8

    def sibling(self):
        return {"dp": self.hi * 2 + 1 - self.core}

    def across(self):
        return {"dp": (1 - self.hi) * 2 + self.core}

    def copy(self, src, dst, kind, recv, to):
        return pltpu.make_async_remote_copy(
            src_ref=src, dst_ref=dst, send_sem=self.sem.at[kind], recv_sem=recv, device_id=to, device_id_type=MESH
        )

    def bufs(self, u):
        if u in Z_FIRST:
            k = Z_FIRST.index(u)
            return self.ys2.at[k], self.yr2.at[k], self.zs2.at[k], self.zr2.at[k]
        k = Y_FIRST.index(u)
        return self.ys.at[k], self.yr.at[k], self.zs.at[k], self.zr.at[k]

    def c_copy(self, u):
        return self.copy(self.cs.at[u], self.cr.at[u], 0, self.csem.at[u], self.sibling())

    def y_copy(self, u):
        ys, yr, _, _ = self.bufs(u)
        return self.copy(ys, yr, 3 if u in Z_FIRST else 1, self.ysem.at[u], self.across())

    def z_start(self, u):
        _, _, zs, zr = self.bufs(u)
        for d in self.FAR_FIRST:
            self.copy(zs.at[self.Z(d)], zr.at[d - 1], 4 if u in Z_FIRST else 2, self.zsem.at[u], {"ctx": self.Z(d)}).start()

    def z_wait(self, u):
        _, _, _, zr = self.bufs(u)
        self.copy(zr, zr, 2, self.zsem.at[u], self.across()).wait_recv()

    def rows(self, u, i, hi, core):
        start = pl.multiple_of((hi * 2 + core) * 128, 128)
        return self.grad[u * UH + i, pl.ds(start, 128), :].reshape(8, 16, 128)

    def both(self, u, i, hi):
        return self.rows(u, i, hi, self.core) + self.cr[u, hi, :, i].astype(jnp.float32)

    def mine(self, u, i, hi):
        start = pl.multiple_of((hi * 2 + self.core) * 128 + self.z * 16, 16)
        return self.grad[u * UH + i, pl.ds(start, 16), :] + self.cr[u, hi, self.z, i].astype(jnp.float32)

    def a(self, u):
        for hi in range(2):
            for i in range(UH):
                self.cs[u, hi, :, i] = self.rows(u, i, hi, 1 - self.core).astype(jnp.bfloat16)
        self.c_copy(u).start()

    def b(self, u):
        self.c_copy(u).wait_recv()
        ys, _, zs, _ = self.bufs(u)
        for i in range(UH):
            if u in Z_FIRST:
                for hi in range(2):
                    zs[:, hi, i] = self.both(u, i, hi).astype(jnp.bfloat16)
            else:
                ys[:, i] = self.both(u, i, 1 - self.hi).astype(jnp.bfloat16)
        if u in Z_FIRST:
            self.z_start(u)
        else:
            self.y_copy(u).start()

    def c(self, u):
        ys, yr, zs, zr = self.bufs(u)
        if u in Z_FIRST:
            self.z_wait(u)
            k = Z_FIRST.index(u)
            for i in range(UH):
                for far in range(2):
                    hi = 1 - self.hi if far else self.hi
                    total = self.mine(u, i, hi)
                    for d in range(7):
                        total = total + zr[d, hi, i].astype(jnp.float32)
                    if far:
                        ys[i] = total.astype(jnp.bfloat16)
                    else:
                        self.acc[k, i] = total
            self.y_copy(u).start()
        else:
            self.y_copy(u).wait_recv()
            for i in range(UH):
                zs[:, i] = (self.both(u, i, self.hi) + yr[:, i].astype(jnp.float32)).astype(jnp.bfloat16)
            self.z_start(u)

    def d(self, u):
        _, yr, _, zr = self.bufs(u)
        if u in Z_FIRST:
            self.y_copy(u).wait_recv()
        else:
            self.z_wait(u)
        for i in range(UH):
            if u in Z_FIRST:
                total = self.acc[Z_FIRST.index(u), i] + yr[i].astype(jnp.float32)
            else:
                total = self.mine(u, i, self.hi) + yr[self.z, i].astype(jnp.float32)
                for d in range(7):
                    total = total + zr[d, i].astype(jnp.float32)
            self.fin[u * UH + i] = total

    def drain(self):
        for kind, whole in enumerate((self.cs, self.ys, self.zr, self.ys2, self.zr2)):
            self.copy(whole, whole, kind, self.csem.at[0], self.across()).wait_send()

    def scratch():
        tile, half = (UH, 16, 128), (2, UH, 16, 128)
        ny, nz = len(Y_FIRST), len(Z_FIRST)
        shapes = [(NU, 2, 8) + tile] * 2 + [(ny, 8) + tile] * 3 + [(ny, 7) + tile, (nz, 8) + half, (nz, 7) + half, (nz,) + tile, (nz,) + tile]
        return [
            pltpu.VMEM((16, 16, 128), jnp.float32),
            *(pltpu.VMEM(shape, jnp.bfloat16) for shape in shapes),
            pltpu.VMEM((nz,) + tile, jnp.float32),
            pltpu.SemaphoreType.DMA((5,)),
            *[pltpu.SemaphoreType.DMA((NU,))] * 3,
        ]


def start_of_doc(pos, lengths):
    end, low = jnp.int32(0), jnp.zeros_like(pos)
    for d in range(8):
        n = lengths[0, d]
        end = end + n
        low = low + jnp.where(pos >= end, n, 0)
    return low


class Attend:
    def __init__(self, order, lengths, q, qr, qt, keys, window, turned, bias, u):
        self.order, self.lengths, self.q, self.qr, self.qt, self.keys, self.window, self.turned, self.bias, self.u = order, lengths, q, qr, qt, keys, window, turned, bias, u
        self.firsts = []

    def arrange(self):
        lane = lax.broadcasted_iota(jnp.int32, (BLOCK, 128), 1)
        for b in range(3):
            rows = slice(b * BLOCK, (b + 1) * BLOCK)
            for c in range(4):
                cols = slice(c * 128, (c + 1) * 128)
                self.qt[b, :, :, cols] = jnp.swapaxes(self.q[0, rows, :, cols], 0, 1)
            for j in range(8):
                pair = self.qr[0, rows, j * 128 : (j + 1) * 128]
                zero = jnp.zeros_like(pair)
                self.qt[b, 2 * j, :, 512:640] = jnp.where(lane < 64, pair, zero)
                self.qt[b, 2 * j + 1, :, 512:640] = jnp.where(lane < 64, zero, pair)

    def mask(self):
        place = lax.axis_index("ctx")
        for b in range(3):
            block = self.order[0, place * 3 + b]
            first = jnp.maximum(block - 6, 0) * BLOCK
            self.firsts.append(jnp.maximum(block - 6, 0) * 8)
            pos = block * BLOCK + lax.broadcasted_iota(jnp.int32, (BLOCK, 1), 0)
            low = start_of_doc(pos, self.lengths)
            j = first + lax.broadcasted_iota(jnp.int32, (BLOCK, SPAN), 1)
            self.bias[b] = jnp.where((j >= low) & (j <= pos), 0.0, -1e30)

    def windows(self):
        for b in range(3):
            k = self.keys[pl.ds(self.firsts[b], SPAN // 8)].reshape(SPAN, 640)
            self.window[b] = k
            self.turned[b] = k.T

    def block(self, head, n, b):
        q = self.qt[b, pl.ds(head, n)].reshape(n * BLOCK, 640)
        k = self.window[b]
        s = jnp.dot(q, self.turned[b], preferred_element_type=jnp.float32)
        s = s.reshape(n, BLOCK, SPAN) + self.bias[b][None]
        top = jnp.max(s, axis=2, keepdims=True)
        p = jnp.exp2((s - top) * SCALE)
        total = jnp.sum(p, axis=2, keepdims=True)
        weights = p.astype(jnp.bfloat16).reshape(n * BLOCK, SPAN)
        mixed = lax.dot_general(weights, k[:, :512], (((1,), (0,)), ((), ())), preferred_element_type=jnp.float32)
        self.u[pl.ds(head, n), b * BLOCK : (b + 1) * BLOCK, :] = (mixed.reshape(n, BLOCK, 512) / total).astype(jnp.bfloat16)


def kernel(order_hbm, lengths_hbm, lat_hbm, rope_hbm, q_hbm, qr_hbm, do_hbm, w_hbm, attn, out, order, lengths, lat, rope, q, qr, do, w, loads, keys, send, recv, qt, window, turned, bias, u, grad, *reduce_refs):
    copies = [
        pltpu.make_async_copy(src, dst, loads.at[i])
        for i, (src, dst) in enumerate(
            ((lat_hbm, lat), (rope_hbm, rope), (order_hbm, order), (lengths_hbm, lengths), (q_hbm, q), (qr_hbm, qr), (do_hbm, do), (w_hbm, w))
        )
    ]
    g = Gather(keys, send, recv)
    r = Reduce(grad, *reduce_refs)
    barrier = pltpu.get_barrier_semaphore()
    partners = g.partners() + [r.sibling(), r.across()]
    for t in partners:
        pl.semaphore_signal(barrier, inc=1, device_id=t, device_id_type=MESH)
    for c in copies:
        c.start()
    copies[0].wait()
    copies[1].wait()
    mine = ((g.z * 2 + g.y) * 4 + g.x) * 3
    twice = jnp.concatenate([rope[0], rope[0]], axis=1)
    for t in range(3):
        keys[mine + t, :, 0:512] = lat[0, t * 8 : (t + 1) * 8, :]
        keys[mine + t, :, 512:640] = twice[t * 8 : (t + 1) * 8, :]
    pl.semaphore_wait(barrier, len(partners))
    g.begin()
    for c in copies[2:]:
        c.wait()
    a = Attend(order, lengths, q, qr, qt, keys, window, turned, bias, u)
    a.arrange()
    a.mask()
    g.run()
    a.windows()

    def gradient(first, n):
        for h in range(n):
            col = pl.ds(pl.multiple_of((first + h) * 128, 128), 128)
            grad[first + h] = lax.dot_general(u[first + h], do[0, :, col], (((0,), (0,)), ((), ())), preferred_element_type=jnp.float32)

    def group(first, n, work, units):
        for b in range(3):
            a.block(first, n, b)
            for act, u in work[b]:
                act(u)
        gradient(first, n)
        for u in units:
            r.a(u)

    none = ()
    group(0, 6, (none, none, none), (1, 0, 2))
    group(6, 6, (((r.b, 1), (r.b, 0), (r.b, 2)), none, none), (4, 3, 5))
    group(12, 4, (none, ((r.b, 4), (r.b, 3), (r.b, 5)), none), (6, 7))

    def values(i):
        def head(h, _):
            col = pl.ds(pl.multiple_of(h * 128, 128), 128)
            attn[0, :, col] = jnp.dot(u[h], w[h], preferred_element_type=jnp.float32).astype(jnp.bfloat16)
            return 0

        lax.fori_loop(i * GH, (i + 1) * GH, head, 0)

    values(0)
    for unit in (6, 7):
        r.b(unit)
    for unit in (1, 2):
        r.c(unit)
    values(1)
    for unit in (0, 4, 5):
        r.c(unit)
    values(2)
    for unit in (6, 7, 3):
        r.c(unit)
    values(3)
    for unit in (1, 2, 4, 5, 0, 6, 3, 7):
        r.d(unit)
    out[...] = jnp.swapaxes(r.fin[...], 0, 1)
    g.drain()
    r.drain()


def on_device(q_lat, q_rope, latent, k_rope, d_out, w_uv, doc_lengths, block_order):
    hbm = pl.BlockSpec(memory_space=pltpu.HBM)
    vmem = pl.BlockSpec(memory_space=pltpu.VMEM)
    operands = (block_order, doc_lengths, latent, k_rope, q_lat, q_rope, d_out, w_uv)
    return pl.pallas_call(
        kernel,
        out_shape=[pltpu.VMEM((1, 192, 2048), jnp.bfloat16), pltpu.VMEM((16, 16, 128), jnp.float32)],
        in_specs=[hbm] * 8,
        out_specs=[vmem, vmem],
        scratch_shapes=[
            pltpu.SMEM((1, 24), jnp.int32),
            pltpu.SMEM((1, 8), jnp.int32),
            *(pltpu.VMEM(x.shape, x.dtype) for x in operands[2:]),
            pltpu.SemaphoreType.DMA((8,)),
            pltpu.VMEM((192, 8, 640), jnp.bfloat16),
            pltpu.SemaphoreType.DMA((3,)),
            pltpu.SemaphoreType.DMA((Gather.COUNT,)),
            pltpu.VMEM((3, 16, BLOCK, 640), jnp.bfloat16),
            pltpu.VMEM((3, SPAN, 640), jnp.bfloat16),
            pltpu.VMEM((3, 640, SPAN), jnp.bfloat16),
            pltpu.VMEM((3, BLOCK, SPAN), jnp.float32),
            pltpu.VMEM((16, 192, 512), jnp.bfloat16),
            pltpu.VMEM((16, 512, 128), jnp.float32),
            *Reduce.scratch(),
        ],
        compiler_params=pltpu.CompilerParams(collective_id=0, has_side_effects=True, vmem_limit_bytes=VMEM_MB << 20),
        name="attention",
    )(*operands)


def solution(mesh):
    return jax.shard_map(
        on_device,
        mesh=mesh,
        in_specs=(
            P("dp", "ctx", "tp", None),
            P("dp", "ctx", "tp"),
            P("dp", ("ctx", "tp"), None),
            P("dp", ("ctx", "tp"), None),
            P("dp", "ctx", "tp"),
            P("tp", None, None),
            P("dp", None),
            P("dp", None),
        ),
        out_specs=(P("dp", "ctx", "tp"), P(("dp", "ctx"), "tp", None)),
        check_vma=False,
    )
```
